256 devices in a mesh: queue: 32 (over x_hi, z, core), mp: 8 (over x_lo, y).
Axes of the slice: x: 4 (x_hi: 2, x_lo: 2; x = x_hi * 2 + x_lo), y: 4, z: 8, core: 2. Of those that a mesh axis runs over, the one named last changes fastest.
Arguments:
- speech: bfloat16 [24576, 1024], P(('queue', 'mp')), may hold values from -6 to 6
- weight: bfloat16 [1024, 1024], P(None, 'mp'), may hold values from -0.1875 to 0.1875
- norm_gain: float32 [1024], replicated, may hold values from 0.1 to 1.9
- queue_keys: bfloat16 [24576, 1024], P('queue'), may hold values from -96 to 96
- new_keys: bfloat16 [768, 1024], replicated, may hold values from -6 to 6
- pointer: int32 [1], replicated, may hold values from 0 to 24575
- positives: int32 [24576], P(('queue', 'mp')), may hold values from 0 to 24575
Outputs:
- loss: float32 [24576], P(('queue', 'mp'))
- grad_speech: bfloat16 [24576, 1024], P(('queue', 'mp'))
- queue_next: bfloat16 [24576, 1024], P('queue')
The draws below stay inside these ranges and needn't reach their ends.
All inputs are finite; a program needn't handle non-finite values.
Results may differ from the reference program's by a relative error of at most 0.022.
The reference program's roundings to bfloat16 on the way (of `queries`, `weights` and `hidden_grad`) count: a program that leaves them out, or rounds other values in their place, can miss the bound.
Values may be sent and summed in bfloat16 or wider, within the bound.
No kernel may reach another device: no remote copies, remote signals or barrier semaphores. Data moves between devices by JAX's collectives and lax.ppermute only.
A program may use at most 128 MiB of HBM per device.

```python
import math
import jax
import jax.numpy as jnp
from jax import lax

D = 1024
KEY_DEV = 768
QUERIES = 24576
QUEUE = 24576
N_QUEUE = 32


def draw_queue_keys(key, part):
    key = jax.random.fold_in(key, 7)
    entry_key = jax.random.fold_in(key, 0)
    values = jax.random.normal(entry_key, (QUEUE, D), jnp.float32)
    return values.astype(jnp.bfloat16)


def touch_ends(array, stream_key, smallest, top_value):
    extent = array.shape
    spot = [jax.random.randint(jax.random.fold_in(stream_key, axis), (), 0, extent[axis]) for axis in range(len(extent))]
    array = array.at[tuple(spot)].set(smallest)
    longest = extent.index(max(extent))
    spot[longest] = (spot[longest] + 1) % extent[longest]
    return array.at[tuple(spot)].set(top_value)


def level_of(key, shape, cuts, least, high):
    def one(position, parts):
        heights = jax.random.uniform(jax.random.fold_in(jax.random.fold_in(key, 6), position), (parts,), jnp.float32, least / len(cuts), high / len(cuts))
        return jnp.repeat(jnp.exp(heights), shape[position] // parts).reshape((-1,) + (1,) * (len(shape) - position - 1))

    loudness = one(*cuts[0])
    for cut in cuts[1:]:
        loudness = loudness * one(*cut)
    return loudness


def gaussian(stream_key, shape, spread, limit, cuts=(), held_as=jnp.bfloat16):
    result = spread * jax.random.normal(stream_key, shape, jnp.float32)
    if cuts:
        result = result * level_of(stream_key, shape, cuts, -0.22, 0.18)
    return jnp.clip(result, -limit, limit).astype(held_as)


def setup_inputs(seed: int = 0) -> dict:
    seeds = jax.random.split(jax.random.key(seed), 8)
    speech = gaussian(seeds[0], (QUERIES, D), 1.0, 6.0, ((0, 256),))
    weight = gaussian(seeds[1], (D, D), D ** -0.5, 0.1875, ((1, 8),))
    norm_gain = jnp.clip(1.0 + 0.18 * jax.random.normal(seeds[2], (D,), jnp.float32), 0.1, 1.9)
    queue_keys = draw_queue_keys(jax.random.fold_in(seeds[7], 71), 0)
    new_keys = gaussian(seeds[4], (KEY_DEV, D), 1.0, 6.0)
    pointer = jax.random.randint(seeds[5], (1,), 0, QUEUE).astype(jnp.int32)
    positives = touch_ends(jax.random.randint(seeds[6], (QUERIES,), 0, QUEUE), jax.random.fold_in(seeds[6], 1), 0, QUEUE - 1).astype(jnp.int32)
    return dict(speech=speech, weight=weight, norm_gain=norm_gain, queue_keys=queue_keys, new_keys=new_keys, pointer=pointer, positives=positives)


def reference(speech, weight, norm_gain, queue_keys, new_keys, pointer, positives):
    hidden = jnp.dot(speech, weight, preferred_element_type=jnp.float32)
    inverse_rms = lax.rsqrt(lax.optimization_barrier(jnp.mean(hidden * hidden, axis=1, keepdims=True)) + 1e-06)
    queries = (hidden * inverse_rms * norm_gain).astype(jnp.bfloat16)
    factor = 2.0 / math.sqrt(D)
    blocks = queue_keys.reshape(N_QUEUE, KEY_DEV, D)
    block_ids = jnp.arange(N_QUEUE, dtype=jnp.int32)
    column_ids = jnp.arange(KEY_DEV, dtype=jnp.int32)

    def block_scores(key_rows, block_id):
        scores = lax.dot_general(queries, key_rows, (((1,), (1,)), ((), ())), preferred_element_type=jnp.float32) * factor
        is_positive = column_ids[None, :] == (positives - block_id * KEY_DEV)[:, None]
        return (scores, is_positive)

    def forward(carry, pieces):
        row_peak, row_total, row_positive = carry
        scores, is_positive = block_scores(pieces[0], pieces[1])
        new_peak = jnp.maximum(row_peak, lax.optimization_barrier(jnp.max(scores, axis=1)))
        row_total = row_total * jnp.exp(row_peak - new_peak) + lax.optimization_barrier(jnp.sum(jnp.exp(scores - new_peak[:, None]), axis=1))
        row_positive = row_positive + lax.optimization_barrier(jnp.sum(jnp.where(is_positive, scores, 0.0), axis=1))
        return ((new_peak, row_total, row_positive), None)
    start_state = (jnp.full((QUERIES,), -1e+30, jnp.float32), jnp.zeros((QUERIES,), jnp.float32), jnp.zeros((QUERIES,), jnp.float32))
    (row_peak, row_total, row_positive), _ = lax.scan(forward, start_state, (blocks, block_ids))
    log_total = row_peak + jnp.log(row_total)
    loss = log_total - row_positive

    def backward(carry, pieces):
        scores, is_positive = block_scores(pieces[0], pieces[1])
        weights = (jnp.exp(scores - log_total[:, None]) - is_positive.astype(jnp.float32)).astype(jnp.bfloat16)
        partial_grad = jnp.dot(weights, pieces[0], preferred_element_type=jnp.float32).astype(jnp.bfloat16)
        partial_grad = lax.optimization_barrier(partial_grad)
        return (carry + partial_grad.astype(jnp.float32), None)
    summed, _ = lax.scan(backward, jnp.zeros((QUERIES, D), jnp.float32), (blocks, block_ids))
    key_grad = summed * (16.0 * factor)
    scaled = norm_gain * key_grad
    cubed = inverse_rms * inverse_rms * inverse_rms
    hidden_grad = (inverse_rms * scaled - hidden * cubed * lax.optimization_barrier(jnp.sum(scaled * hidden, axis=1, keepdims=True)) / D).astype(jnp.bfloat16)
    grad_speech = lax.dot_general(hidden_grad, weight, (((1,), (1,)), ((), ())), preferred_element_type=jnp.float32).astype(jnp.bfloat16)
    row_ids = jnp.arange(QUEUE, dtype=jnp.int32)
    offsets = ((row_ids - pointer[0]) % QUEUE).astype(jnp.int32)
    replaced = offsets < KEY_DEV
    taken = jnp.take(new_keys, jnp.minimum(offsets, KEY_DEV - 1).astype(jnp.int32), axis=0)
    queue_next = jnp.where(replaced[:, None], taken, queue_keys)
    return (loss, grad_speech, queue_next)
```

```python
import functools
import math

import jax
import jax.numpy as jnp
from jax import lax
from jax.experimental import pallas as pl
from jax.experimental.pallas import tpu as pltpu
from jax.sharding import PartitionSpec as P

RING = 8
BIG = 56 * 1024 * 1024
F32 = jnp.float32
BF16 = jnp.bfloat16
GATHER = (0, -1, 1, -2, 2, -3, 3, -4)
REDUCE = (4, -3, 3, -2, 2, -1, 1, 0)


def vmem():
    return pl.BlockSpec(memory_space=pltpu.VMEM)


def smem():
    return pl.BlockSpec(memory_space=pltpu.SMEM)


def queue_perm(move):
    def index(x, z, c):
        return (x * RING + z) * 2 + c

    return [
        (index(x, z, c), index(*move(x, z, c)))
        for x in range(2)
        for z in range(RING)
        for c in range(2)
    ]


UP = queue_perm(lambda x, z, c: (x, (z + 1) % RING, c))
DOWN = queue_perm(lambda x, z, c: (x, (z - 1) % RING, c))
CORE = queue_perm(lambda x, z, c: (x, z, 1 - c))
FAR = queue_perm(lambda x, z, c: (1 - x, z, c))


def score_kernel(factor, rows, place, *refs):
    slots = refs[:RING]
    weights = refs[RING : RING + 8]
    gain = refs[RING + 8]
    keys = refs[RING + 9 : RING + 13]
    probs, stats, wanted, own_hidden, full_weight = refs[RING + 13 : RING + 18]
    speech, hidden, queries, scores, table = refs[RING + 18 :]
    z, mp = place[0], place[1]
    width = hidden.shape[1]
    count = keys[0].shape[0]
    piece = weights[0].shape[1]

    for step in range(8):
        start = pl.multiple_of(jnp.bitwise_xor(mp, step) * piece, piece)
        full_weight[:, pl.ds(start, piece)] = weights[step][...]
    for slot, offset in enumerate(GATHER):
        owner = lax.rem(z + offset + RING, RING)
        start = pl.multiple_of(owner * rows, rows)
        speech[pl.ds(start, rows), :] = slots[slot][:, :width]
        codes = slots[slot][:, width:].astype(F32)
        ids = codes[:, 0:1] * 128.0 + codes[:, 1:2]
        wanted[pl.ds(start, rows), :] = jnp.broadcast_to(ids, (rows, 128))

    tile = 256

    @pl.loop(0, width // tile)
    def _(t):
        columns = pl.ds(pl.multiple_of(t * tile, tile), tile)
        hidden[:, columns] = jnp.dot(
            speech[...], full_weight[:, columns], preferred_element_type=F32
        )

    @pl.loop(0, RING)
    def _(b):
        span = pl.ds(pl.multiple_of(b * rows, rows), rows)
        block = hidden[span, :]
        inverse = lax.rsqrt(jnp.mean(block * block, axis=1, keepdims=True) + 1e-06)
        queries[span, :] = (block * inverse * gain[...]).astype(BF16)

    own_hidden[...] = hidden[pl.ds(pl.multiple_of(z * rows, rows), rows), :]

    for j in range(4):

        @pl.loop(0, count // tile)
        def _(t, j=j):
            key_rows = keys[j][pl.ds(pl.multiple_of(t * tile, tile), tile), :]
            product = lax.dot_general(
                queries[...], key_rows, (((1,), (1,)), ((), ())), preferred_element_type=F32
            )
            start = pl.multiple_of(j * count + t * tile, tile)
            scores[:, pl.ds(start, tile)] = product * factor

    step_rows = 32

    @pl.loop(0, RING * rows // step_rows)
    def _(b):
        span = pl.ds(pl.multiple_of(b * step_rows, step_rows), step_rows)
        block = scores[span, :]
        peak = jnp.max(block, axis=1, keepdims=True)
        powers = jnp.exp(block - peak)
        probs[span, :] = powers.astype(BF16)
        total = jnp.sum(powers, axis=1, keepdims=True)
        ids = wanted[span, :][:, 0:1].astype(jnp.int32)
        found = jnp.zeros((step_rows, 1), F32)
        for j in range(4):
            mine = lax.broadcasted_iota(jnp.int32, (step_rows, count), 1) == ids - place[2 + j]
            found += jnp.sum(
                jnp.where(mine, block[:, j * count : (j + 1) * count], 0.0), axis=1, keepdims=True
            )
        lane = lax.broadcasted_iota(jnp.int32, (step_rows, 128), 1)
        table[span, :] = jnp.where(
            lane == 0, peak, jnp.where(lane == 1, total, jnp.where(lane == 2, found, 0.0))
        )

    stats[...] = table[...].T[:8, :]


def product_kernel(place, probs, wanted, *refs):
    keys, (sums, picked) = refs[:4], refs[4:]
    count = keys[0].shape[0]
    ids = wanted[...][:, 0:1].astype(jnp.int32)
    total = jnp.zeros(sums.shape, F32)
    chosen = jnp.zeros(sums.shape, F32)
    for j in range(4):
        total += jnp.dot(
            probs[:, j * count : (j + 1) * count], keys[j][...], preferred_element_type=F32
        )
        mine = lax.broadcasted_iota(jnp.int32, (probs.shape[0], count), 1) == ids - place[2 + j]
        chosen += jnp.dot(
            mine.astype(F32).astype(BF16), keys[j][...], preferred_element_type=F32
        )
    sums[...] = total
    picked[...] = chosen.astype(BF16)


def scale_kernel(rows, place, sums, picked, local, merged, *refs):
    outs, loss, table = refs[:RING], refs[RING], refs[RING + 1]
    z = place[0]
    log_total = merged[0:1, :] + jnp.log(merged[1:2, :])
    scale = jnp.exp(local[0:1, :] - log_total)
    losses = log_total - merged[2:3, :]
    row = lax.broadcasted_iota(jnp.int32, (128, scale.shape[1]), 0)
    table[...] = jnp.where(row == 0, scale, jnp.where(row == 1, losses, 0.0)).T
    for slot, offset in enumerate(REDUCE):
        start = pl.multiple_of(lax.rem(z + offset + RING, RING) * rows, rows)
        span = pl.ds(start, rows)
        outs[slot][...] = (
            table[span, 0:1] * sums[span, :] - picked[span, :].astype(F32)
        ).astype(BF16)
    loss[...] = table[pl.ds(pl.multiple_of(z * rows, rows), rows), 1:2]


def final_kernel(factor, first, second, own, hidden, gain, weight, out):
    width = hidden.shape[1]
    grad = (first[...].astype(F32) + second[...].astype(F32) + own[...].astype(F32)) * factor
    scaled = gain[...] * grad
    values = hidden[...]
    inverse = lax.rsqrt(jnp.mean(values * values, axis=1, keepdims=True) + 1e-06)
    inner = jnp.sum(scaled * values, axis=1, keepdims=True)
    hidden_grad = (
        inverse * scaled - values * (inverse * inverse * inverse) * inner / width
    ).astype(BF16)
    out[...] = lax.dot_general(
        hidden_grad, weight[...], (((1,), (1,)), ((), ())), preferred_element_type=F32
    ).astype(BF16)


def queue_kernel(shift, keys, fresh, out):
    count = keys.shape[0]
    wanted = lax.broadcasted_iota(jnp.int32, (count, 1), 0) + shift[0]
    pick = lax.broadcasted_iota(jnp.int32, (count, fresh.shape[0]), 1) == wanted
    moved = jnp.dot(pick.astype(F32).astype(BF16), fresh[...], preferred_element_type=F32)
    replaced = (wanted >= 0) & (wanted < fresh.shape[0])
    out[...] = jnp.where(replaced, moved, keys[...].astype(F32)).astype(BF16)


def merge(mine, other):
    peak = jnp.maximum(mine[0:1], other[0:1])
    total = mine[1:2] * jnp.exp(mine[0:1] - peak) + other[1:2] * jnp.exp(other[0:1] - peak)
    found = mine[2:3] + other[2:3]
    row = lax.broadcasted_iota(jnp.int32, mine.shape, 0)
    return jnp.where(row == 0, peak, jnp.where(row == 1, total, found))


def shards(speech, weight, norm_gain, queue_keys, new_keys, pointer, positives):
    rows, width = speech.shape
    count = queue_keys.shape[0]
    total_rows = RING * rows
    queue_length = count * lax.axis_size("queue")
    queue_index = lax.axis_index("queue")
    mp = lax.axis_index("mp")
    z = (queue_index // 2) % RING
    factor = 2.0 / math.sqrt(width)
    params = pltpu.CompilerParams(vmem_limit_bytes=BIG)

    far = lax.ppermute(queue_keys, "queue", FAR)
    near = lax.ppermute(queue_keys, "queue", CORE)
    far_near = lax.ppermute(far, "queue", CORE)
    keys = (queue_keys, near, far, far_near)
    flipped = queue_index ^ (2 * RING)
    bases = [index * count for index in (queue_index, queue_index ^ 1, flipped, flipped ^ 1)]
    place = jnp.stack([z, mp] + bases).astype(jnp.int32)

    codes = jnp.stack([positives // 128, positives % 128], axis=1).astype(BF16)
    packed = jnp.concatenate([speech, jnp.pad(codes, ((0, 0), (0, 126)))], axis=1)
    slots = {0: packed}
    for step in range(1, 5):
        slots[-step] = lax.ppermute(slots[1 - step], "queue", UP)
        if step < 4:
            slots[step] = lax.ppermute(slots[step - 1], "queue", DOWN)
    pieces = [weight] + [
        lax.ppermute(weight, "mp", [(m, m ^ step) for m in range(8)]) for step in range(1, 8)
    ]
    gain = norm_gain.reshape(1, width)

    probs, stats, wanted, own_hidden, full_weight = pl.pallas_call(
        functools.partial(score_kernel, factor, rows),
        out_shape=(
            jax.ShapeDtypeStruct((total_rows, 4 * count), BF16),
            jax.ShapeDtypeStruct((8, total_rows), F32),
            jax.ShapeDtypeStruct((total_rows, 128), F32),
            jax.ShapeDtypeStruct((rows, width), F32),
            jax.ShapeDtypeStruct((width, width), BF16),
        ),
        in_specs=[smem()] + [vmem()] * (RING + 8 + 1 + 4),
        out_specs=(vmem(),) * 5,
        scratch_shapes=[
            pltpu.VMEM((total_rows, width), BF16),
            pltpu.VMEM((total_rows, width), F32),
            pltpu.VMEM((total_rows, width), BF16),
            pltpu.VMEM((total_rows, 4 * count), F32),
            pltpu.VMEM((total_rows, 128), F32),
        ],
        compiler_params=params,
        cost_estimate=pl.CostEstimate(
            flops=2 * total_rows * width * (4 * count + width),
            bytes_accessed=20_000_000,
            transcendentals=total_rows * 4 * count,
        ),
        name="scores",
    )(place, *[slots[offset] for offset in GATHER], *pieces, gain, *keys)

    merged = stats
    for step in (1, 2, 4):
        swap = queue_perm(lambda x, z, c, step=step: (x, z ^ step, c))
        merged = merge(merged, lax.ppermute(merged, "queue", swap))

    tile = 256
    sums, picked = pl.pallas_call(
        product_kernel,
        out_shape=(
            jax.ShapeDtypeStruct((total_rows, width), F32),
            jax.ShapeDtypeStruct((total_rows, width), BF16),
        ),
        grid=(width // tile,),
        in_specs=[
            smem(),
            pl.BlockSpec((total_rows, 4 * count), lambda t: (0, 0)),
            pl.BlockSpec((total_rows, 128), lambda t: (0, 0)),
        ]
        + [pl.BlockSpec((count, tile), lambda t: (0, t))] * 4,
        out_specs=(pl.BlockSpec((total_rows, tile), lambda t: (0, t)),) * 2,
        compiler_params=params,
        cost_estimate=pl.CostEstimate(
            flops=4 * total_rows * width * 4 * count, bytes_accessed=16_000_000, transcendentals=0
        ),
        name="products",
    )(place, probs, wanted, *keys)

    *grads, losses = pl.pallas_call(
        functools.partial(scale_kernel, rows),
        out_shape=[jax.ShapeDtypeStruct((rows, width), BF16)] * RING
        + [jax.ShapeDtypeStruct((rows, 1), F32)],
        in_specs=[smem()] + [vmem()] * 4,
        out_specs=[vmem()] * (RING + 1),
        scratch_shapes=[pltpu.VMEM((total_rows, 128), F32)],
        compiler_params=params,
        cost_estimate=pl.CostEstimate(
            flops=3 * total_rows * width, bytes_accessed=6_000_000, transcendentals=2000
        ),
        name="scaled",
    )(place, sums, picked, stats, merged)
    grads = dict(zip(REDUCE, grads))

    first, second = grads[4], grads[-3]
    for step in range(4):
        first = lax.ppermute(first, "queue", UP)
        if step < 3:
            first = (first.astype(F32) + grads[3 - step].astype(F32)).astype(BF16)
            second = lax.ppermute(second, "queue", DOWN)
            if step < 2:
                second = (second.astype(F32) + grads[step - 2].astype(F32)).astype(BF16)

    grad_speech = pl.pallas_call(
        functools.partial(final_kernel, 16.0 * factor),
        out_shape=jax.ShapeDtypeStruct((rows, width), BF16),
        in_specs=[vmem()] * 6,
        out_specs=vmem(),
        compiler_params=params,
        cost_estimate=pl.CostEstimate(
            flops=2 * rows * width * width, bytes_accessed=3_500_000, transcendentals=rows
        ),
        name="final",
    )(first, second, grads[0], own_hidden, gain, full_weight)

    shift = (queue_index * count - pointer) % queue_length
    shift = jnp.where(shift >= queue_length - count, shift - queue_length, shift)
    queue_next = pl.pallas_call(
        queue_kernel,
        out_shape=jax.ShapeDtypeStruct(queue_keys.shape, BF16),
        in_specs=[smem(), vmem(), vmem()],
        out_specs=vmem(),
        compiler_params=params,
        cost_estimate=pl.CostEstimate(
            flops=2 * count * count * width, bytes_accessed=5_000_000, transcendentals=0
        ),
        name="queue",
    )(shift, queue_keys, new_keys)
    return (losses.reshape(rows), grad_speech, queue_next)


def solution(mesh):
    return jax.shard_map(
        shards,
        mesh=mesh,
        in_specs=(
            P(("queue", "mp"), None),
            P(None, "mp"),
            P(),
            P("queue", None),
            P(),
            P(),
            P(("queue", "mp")),
        ),
        out_specs=(P(("queue", "mp")), P(("queue", "mp"), None), P("queue", None)),
        check_vma=False,
    )
```

```python
import functools
import math

import jax
import jax.numpy as jnp
from jax import lax
from jax.experimental import pallas as pl
from jax.experimental.pallas import tpu as pltpu
from jax.sharding import PartitionSpec as P

RING = 8
BIG = 56 * 1024 * 1024
F32 = jnp.float32
BF16 = jnp.bfloat16
GATHER = (0, -1, 1, -2, 2, -3, 3, -4)
REDUCE = (4, -3, 3, -2, 2, -1, 1, 0)


def vmem():
    return pl.BlockSpec(memory_space=pltpu.VMEM)


def smem():
    return pl.BlockSpec(memory_space=pltpu.SMEM)


def queue_perm(move):
    def index(x, z, c):
        return (x * RING + z) * 2 + c

    return [
        (index(x, z, c), index(*move(x, z, c)))
        for x in range(2)
        for z in range(RING)
        for c in range(2)
    ]


UP = queue_perm(lambda x, z, c: (x, (z + 1) % RING, c))
DOWN = queue_perm(lambda x, z, c: (x, (z - 1) % RING, c))
CORE = queue_perm(lambda x, z, c: (x, z, 1 - c))
FAR = queue_perm(lambda x, z, c: (1 - x, z, c))


def picked_kernel(rows, place, *refs):
    slots, keys, out, chosen = refs[:RING], refs[RING : RING + 4], refs[RING + 4], refs[RING + 5]
    z = place[0]
    width, count = out.shape[1], keys[0].shape[0]
    for slot, offset in enumerate(GATHER):
        start = pl.multiple_of(lax.rem(z + offset + RING, RING) * rows, rows)
        codes = slots[slot][:, width:].astype(F32)
        ids = (codes[:, 0:1] * 128.0 + codes[:, 1:2]).astype(jnp.int32)
        for j in range(4):
            mine = lax.broadcasted_iota(jnp.int32, (rows, count), 1) == ids - place[3 + j]
            chosen[pl.ds(start, rows), j * count : (j + 1) * count] = mine.astype(F32).astype(BF16)
    tile = 256

    @pl.loop(0, width // tile)
    def _(t):
        columns = pl.ds(pl.multiple_of(t * tile, tile), tile)
        total = jnp.zeros((out.shape[0], tile), F32)
        for j in range(4):
            total += jnp.dot(
                chosen[:, j * count : (j + 1) * count],
                keys[j][:, columns],
                preferred_element_type=F32,
            )
        out[:, columns] = total.astype(BF16)


def score_kernel(factor, rows, place, *refs):
    slots = refs[:RING]
    mine_weight, other_weight, gain = refs[RING : RING + 3]
    keys = refs[RING + 3 : RING + 7]
    outs = refs[RING + 7 : 2 * RING + 7]
    own_hidden, full_weight = refs[2 * RING + 7 : 2 * RING + 9]
    speech, hidden, queries, scores, probs, wanted, peaks, table = refs[2 * RING + 9 :]
    z, core = place[0], place[2]
    width = hidden.shape[1]
    count = keys[0].shape[0]
    piece = mine_weight.shape[1]
    half = mine_weight.shape[0] // 8

    for m in range(8):
        columns = slice(m * piece, (m + 1) * piece)
        block = slice(m * half, (m + 1) * half)
        full_weight[pl.ds(pl.multiple_of(core * half, half), half), columns] = mine_weight[block, :]
        full_weight[pl.ds(pl.multiple_of((1 - core) * half, half), half), columns] = other_weight[
            block, :
        ]
    for slot, offset in enumerate(GATHER):
        owner = lax.rem(z + offset + RING, RING)
        start = pl.multiple_of(owner * rows, rows)
        speech[pl.ds(start, rows), :] = slots[slot][:, :width]
        codes = slots[slot][:, width:].astype(F32)
        ids = codes[:, 0:1] * 128.0 + codes[:, 1:2]
        wanted[pl.ds(start, rows), :] = jnp.broadcast_to(ids, (rows, 128))

    tile = 256

    @pl.loop(0, width // tile)
    def _(t):
        columns = pl.ds(pl.multiple_of(t * tile, tile), tile)
        hidden[:, columns] = jnp.dot(
            speech[...], full_weight[:, columns], preferred_element_type=F32
        )

    @pl.loop(0, RING)
    def _(b):
        span = pl.ds(pl.multiple_of(b * rows, rows), rows)
        block = hidden[span, :]
        inverse = lax.rsqrt(jnp.mean(block * block, axis=1, keepdims=True) + 1e-06)
        queries[span, :] = (block * inverse * gain[...]).astype(BF16)

    own_hidden[...] = hidden[pl.ds(pl.multiple_of(z * rows, rows), rows), :]
    peaks[...] = jnp.full(peaks.shape, -3e38, F32)

    for j in range(4):

        @pl.loop(0, count // tile)
        def _(t, j=j):
            key_rows = keys[j][pl.ds(pl.multiple_of(t * tile, tile), tile), :]
            product = (
                lax.dot_general(
                    queries[...], key_rows, (((1,), (1,)), ((), ())), preferred_element_type=F32
                )
                * factor
            )
            start = pl.multiple_of(j * count + t * tile, tile)
            scores[:, pl.ds(start, tile)] = product
            peaks[...] = jnp.maximum(
                peaks[...], jnp.maximum(product[:, :128], product[:, 128:])
            )

    step_rows = 32

    @pl.loop(0, RING * rows // step_rows)
    def _(b):
        span = pl.ds(pl.multiple_of(b * step_rows, step_rows), step_rows)
        peak = jnp.max(peaks[span, :], axis=1, keepdims=True).astype(BF16).astype(F32)
        ids = wanted[span, 0:1].astype(jnp.int32)
        partial = jnp.zeros((step_rows, 128), F32)
        for j in range(4):
            mine = lax.broadcasted_iota(jnp.int32, (step_rows, count), 1) == ids - place[3 + j]
            powers = jnp.exp(scores[span, j * count : (j + 1) * count] - peak)
            powers = jnp.where(mine, 0.0, powers)
            probs[span, j * count : (j + 1) * count] = powers.astype(BF16)
            for g in range(count // 128):
                partial += powers[:, g * 128 : (g + 1) * 128]
        total = jnp.sum(partial, axis=1, keepdims=True)
        table[span, :] = tail(peak, total)

    @pl.loop(0, width // tile)
    def _(t):
        columns = pl.ds(pl.multiple_of(t * tile, tile), tile)
        total = jnp.zeros((RING * rows, tile), F32)
        for j in range(4):
            total += jnp.dot(
                probs[:, j * count : (j + 1) * count],
                keys[j][:, columns],
                preferred_element_type=F32,
            )
        hidden[:, columns] = total

    for slot, offset in enumerate(REDUCE):
        start = pl.multiple_of(lax.rem(z + offset + RING, RING) * rows, rows)
        outs[slot][:, :width] = hidden[pl.ds(start, rows), :].astype(BF16)
        outs[slot][:, width:] = table[pl.ds(start, rows), :]


def tail(peak, total):
    lane = lax.broadcasted_iota(jnp.int32, (peak.shape[0], 128), 1)
    high = total.astype(BF16).astype(F32)
    columns = jnp.where(lane == 0, peak, jnp.where(lane == 1, high, total - high))
    return jnp.where(lane < 3, columns, 0.0).astype(BF16)


def split(block, width):
    end = block[:, width:].astype(F32)
    return (block[:, :width].astype(F32), end[:, 0:1], end[:, 1:2] + end[:, 2:3])


def join(first, second):
    peak = jnp.maximum(first[1], second[1])
    left, right = jnp.exp(first[1] - peak), jnp.exp(second[1] - peak)
    return (first[0] * left + second[0] * right, peak, first[2] * left + second[2] * right)


def merge_kernel(width, first, second, out):
    sums, peak, total = join(split(first[...], width), split(second[...], width))
    out[:, :width] = sums.astype(BF16)
    out[:, width:] = tail(peak, total)


def final_kernel(factor, first, second, own, hidden, gain, picked, weight, out, loss):
    width = hidden.shape[1]
    merged = join(split(first[...], width), split(second[...], width))
    sums, peak, total = join(merged, split(own[...], width))
    values = hidden[...]
    inverse = lax.rsqrt(jnp.mean(values * values, axis=1, keepdims=True) + 1e-06)
    queries = (values * inverse * gain[...]).astype(BF16).astype(F32)
    positive = picked[...].astype(F32)
    score = jnp.sum(queries * positive, axis=1, keepdims=True) * factor
    top = jnp.maximum(peak, score)
    others = jnp.exp(peak - top)
    whole = total * others + jnp.exp(score - top)
    loss[...] = top + jnp.log(whole) - score
    share = others / whole
    grad = (sums * share - positive * (total * share)) * (16.0 * factor)
    scaled = gain[...] * grad
    inner = jnp.sum(scaled * values, axis=1, keepdims=True)
    hidden_grad = (
        inverse * scaled - values * (inverse * inverse * inverse) * inner / width
    ).astype(BF16)
    out[...] = lax.dot_general(
        hidden_grad, weight[...], (((1,), (1,)), ((), ())), preferred_element_type=F32
    ).astype(BF16)


def queue_kernel(shift, keys, fresh, out):
    count = keys.shape[0]
    wanted = lax.broadcasted_iota(jnp.int32, (count, 1), 0) + shift[0]
    pick = lax.broadcasted_iota(jnp.int32, (count, fresh.shape[0]), 1) == wanted
    moved = jnp.dot(pick.astype(F32).astype(BF16), fresh[...], preferred_element_type=F32)
    replaced = (wanted >= 0) & (wanted < fresh.shape[0])
    out[...] = jnp.where(replaced, moved, keys[...].astype(F32)).astype(BF16)


def shards(speech, weight, norm_gain, queue_keys, new_keys, pointer, positives):
    rows, width = speech.shape
    count = queue_keys.shape[0]
    total_rows = RING * rows
    queue_length = count * lax.axis_size("queue")
    queue_index = lax.axis_index("queue")
    mp = lax.axis_index("mp")
    z = (queue_index // 2) % RING
    factor = 2.0 / math.sqrt(width)
    params = pltpu.CompilerParams(vmem_limit_bytes=BIG)

    core = queue_index % 2
    far = lax.ppermute(queue_keys, "queue", FAR)
    near = lax.ppermute(queue_keys, "queue", CORE)
    flipped = queue_index ^ (2 * RING)
    bases = [index * count for index in (queue_index, queue_index ^ 1, flipped, flipped ^ 1)]
    place = jnp.stack([z, mp, core] + bases).astype(jnp.int32)

    codes = jnp.stack([positives // 128, positives % 128], axis=1).astype(BF16)
    packed = jnp.concatenate([speech, jnp.pad(codes, ((0, 0), (0, 126)))], axis=1)
    half = width // 2
    part = lax.dynamic_slice_in_dim(weight, core * half, half, 0)
    part, packed = lax.optimization_barrier((part, packed))
    slots = {0: packed}
    for step in range(1, 5):
        slots[-step] = lax.ppermute(slots[1 - step], "queue", UP)
        if step < 4:
            slots[step] = lax.ppermute(slots[step - 1], "queue", DOWN)
            slots[-step], slots[step] = lax.optimization_barrier((slots[-step], slots[step]))
    mine_weight = lax.all_gather(part, "mp", axis=0, tiled=True)
    far, mine_weight, slots[-4] = lax.optimization_barrier((far, mine_weight, slots[-4]))
    far_near = lax.ppermute(far, "queue", CORE)
    other_weight = lax.ppermute(mine_weight, "queue", CORE)
    far_near, other_weight = lax.optimization_barrier((far_near, other_weight))
    keys = (queue_keys, near, far, far_near)

    gain = norm_gain.reshape(1, width)
    gathered = [slots[offset] for offset in GATHER]

    picked = pl.pallas_call(
        functools.partial(picked_kernel, rows),
        out_shape=jax.ShapeDtypeStruct((total_rows, width), BF16),
        in_specs=[smem()] + [vmem()] * (RING + 4),
        out_specs=vmem(),
        scratch_shapes=[pltpu.VMEM((total_rows, 4 * count), BF16)],
        compiler_params=params,
        cost_estimate=pl.CostEstimate(
            flops=2 * total_rows * width * 4 * count, bytes_accessed=10_000_000, transcendentals=0
        ),
        name="picked",
    )(place, *gathered, *keys)
    groups = [
        [(x * RING + k) * 2 + c for k in range(RING)] for x in range(2) for c in range(2)
    ]
    own_picked = lax.psum_scatter(
        picked, "queue", scatter_dimension=0, axis_index_groups=groups, tiled=True
    )

    block = jax.ShapeDtypeStruct((rows, width + 128), BF16)
    *grads, own_hidden, full_weight = pl.pallas_call(
        functools.partial(score_kernel, factor, rows),
        out_shape=[block] * RING
        + [
            jax.ShapeDtypeStruct((rows, width), F32),
            jax.ShapeDtypeStruct((width, width), BF16),
        ],
        in_specs=[smem()] + [vmem()] * (RING + 3 + 4),
        out_specs=[vmem()] * (RING + 2),
        scratch_shapes=[
            pltpu.VMEM((total_rows, width), BF16),
            pltpu.VMEM((total_rows, width), F32),
            pltpu.VMEM((total_rows, width), BF16),
            pltpu.VMEM((total_rows, 4 * count), F32),
            pltpu.VMEM((total_rows, 4 * count), BF16),
            pltpu.VMEM((total_rows, 128), F32),
            pltpu.VMEM((total_rows, 128), F32),
            pltpu.VMEM((total_rows, 128), BF16),
        ],
        compiler_params=params,
        cost_estimate=pl.CostEstimate(
            flops=2 * total_rows * width * (8 * count + width),
            bytes_accessed=16_000_000,
            transcendentals=total_rows * 4 * count,
        ),
        name="scores",
    )(place, *gathered, mine_weight, other_weight, gain, *keys)
    grads = dict(zip(REDUCE, grads))

    def merge(first, second):
        return pl.pallas_call(
            functools.partial(merge_kernel, width),
            out_shape=block,
            in_specs=[vmem()] * 2,
            out_specs=vmem(),
            compiler_params=params,
            cost_estimate=pl.CostEstimate(
                flops=4 * rows * width, bytes_accessed=600_000, transcendentals=2 * rows
            ),
            name="merge",
        )(first, second)

    first, second = grads[4], grads[-3]
    for step in range(4):
        first = lax.ppermute(first, "queue", UP)
        if step < 3:
            first = merge(first, grads[3 - step])
            second = lax.ppermute(second, "queue", DOWN)
            if step < 2:
                second = merge(second, grads[step - 2])

    grad_speech, losses = pl.pallas_call(
        functools.partial(final_kernel, factor),
        out_shape=(
            jax.ShapeDtypeStruct((rows, width), BF16),
            jax.ShapeDtypeStruct((rows, 1), F32),
        ),
        in_specs=[vmem()] * 7,
        out_specs=(vmem(),) * 2,
        compiler_params=params,
        cost_estimate=pl.CostEstimate(
            flops=2 * rows * width * width, bytes_accessed=3_500_000, transcendentals=rows
        ),
        name="final",
    )(first, second, grads[0], own_hidden, gain, own_picked, full_weight)

    shift = (queue_index * count - pointer) % queue_length
    shift = jnp.where(shift >= queue_length - count, shift - queue_length, shift)
    queue_next = pl.pallas_call(
        queue_kernel,
        out_shape=jax.ShapeDtypeStruct(queue_keys.shape, BF16),
        in_specs=[smem(), vmem(), vmem()],
        out_specs=vmem(),
        compiler_params=params,
        cost_estimate=pl.CostEstimate(
            flops=2 * count * count * width, bytes_accessed=5_000_000, transcendentals=0
        ),
        name="queue",
    )(shift, queue_keys, new_keys)
    return (losses.reshape(rows), grad_speech, queue_next)


def solution(mesh):
    return jax.shard_map(
        shards,
        mesh=mesh,
        in_specs=(
            P(("queue", "mp"), None),
            P(None, "mp"),
            P(),
            P("queue", None),
            P(),
            P(),
            P(("queue", "mp")),
        ),
        out_specs=(P(("queue", "mp")), P(("queue", "mp"), None), P("queue", None)),
        check_vma=False,
    )
```

```python
import functools
import math

import jax
import jax.numpy as jnp
from jax import lax
from jax.experimental import pallas as pl
from jax.experimental.pallas import tpu as pltpu
from jax.sharding import PartitionSpec as P

RING = 8
BLOCK = 256
F32 = jnp.float32
BF16 = jnp.bfloat16
GATHER = (0, -1, 1, -2, 2, -3, 3, -4)
REDUCE = (4, -3, 3, -2, 2, -1, 1, 0)


def limit(mib):
    return pltpu.CompilerParams(vmem_limit_bytes=mib * 1024 * 1024)


def vmem():
    return pl.BlockSpec(memory_space=pltpu.VMEM)


def anywhere():
    return pl.BlockSpec(memory_space=pl.ANY)


def smem():
    return pl.BlockSpec(memory_space=pltpu.SMEM)


def queue_perm(move):
    def index(x, z, c):
        return (x * RING + z) * 2 + c

    return [
        (index(x, z, c), index(*move(x, z, c)))
        for x in range(2)
        for z in range(RING)
        for c in range(2)
    ]


UP = queue_perm(lambda x, z, c: (x, (z + 1) % RING, c))
DOWN = queue_perm(lambda x, z, c: (x, (z - 1) % RING, c))
CORE = queue_perm(lambda x, z, c: (x, z, 1 - c))
FAR = queue_perm(lambda x, z, c: (1 - x, z, c))


def start_keys(sources, held, sems):
    copies = [
        pltpu.make_async_copy(source, held.at[j], sems.at[j]) for j, source in enumerate(sources)
    ]
    for copy in copies:
        copy.start()
    return copies


def unpack_ids(rows, width, z, slots, wanted):
    for slot, offset in enumerate(GATHER):
        start = pl.multiple_of(lax.rem(z + offset + RING, RING) * rows, rows)
        codes = slots[slot][:, width:].astype(F32)
        ids = codes[:, 0:1] * 128.0 + codes[:, 1:2]
        wanted[pl.ds(start, rows), :] = jnp.broadcast_to(ids, (rows, 128))


def picked_kernel(rows, place, *refs):
    slots, keys, out = refs[:RING], refs[RING : RING + 4], refs[RING + 4]
    held, wanted, chosen, sems = refs[RING + 5 :]
    width, count = out.shape[1], held.shape[1]
    copies = start_keys(keys, held, sems)
    unpack_ids(rows, width, place[0], slots, wanted)
    lane = lax.broadcasted_iota(jnp.int32, (BLOCK, 128), 1)
    for b in range(RING * rows // BLOCK):
        span = slice(b * BLOCK, (b + 1) * BLOCK)
        ids = wanted[span, 0:1].astype(jnp.int32)
        total = None
        for j in range(4):
            local = ids - place[3 + j]
            for g in range(count // 128):
                mine = lane == local - g * 128
                start = j * count + g * 128
                chosen[span, start : start + 128] = mine.astype(F32).astype(BF16)
            if b == 0:
                copies[j].wait()
            part = jnp.dot(
                chosen[span, j * count : (j + 1) * count], held[j], preferred_element_type=F32
            )
            total = part if total is None else total + part
        out[span, :] = total.astype(BF16)


def score_kernel(factor, rows, place, *refs):
    slots = refs[:RING]
    own_weight, near_weight, gain = refs[RING], refs[RING + 1 : RING + 6], refs[RING + 6]
    keys = refs[RING + 7 : RING + 11]
    outs = refs[RING + 11 : 2 * RING + 11]
    own_hidden, full_weight = refs[2 * RING + 11 : 2 * RING + 13]
    speech, hidden, queries, scores, probs, wanted, peaks, table, held, sems = refs[2 * RING + 13 :]
    z, mp, core = place[0], place[1], place[2]
    width = hidden.shape[1]
    count = held.shape[1]
    piece = own_weight.shape[1]
    copies = start_keys(keys, held, sems)

    def put(step, values):
        start = pl.multiple_of(jnp.bitwise_xor(mp, step) * piece, piece)
        full_weight[:, pl.ds(start, piece)] = values

    put(0, own_weight[...])
    put(4, near_weight[3][...])
    for i in range(3):
        put(i + 1 + 4 * core, near_weight[i][...])
        put(i + 1 + 4 * (1 - core), near_weight[4][i * width : (i + 1) * width, :])
    for slot, offset in enumerate(GATHER):
        start = pl.multiple_of(lax.rem(z + offset + RING, RING) * rows, rows)
        speech[pl.ds(start, rows), :] = slots[slot][:, :width]
    unpack_ids(rows, width, z, slots, wanted)

    hidden[...] = jnp.dot(speech[...], full_weight[...], preferred_element_type=F32)

    @pl.loop(0, RING)
    def _(b):
        span = pl.ds(pl.multiple_of(b * rows, rows), rows)
        block = hidden[span, :]
        inverse = lax.rsqrt(jnp.mean(block * block, axis=1, keepdims=True) + 1e-06)
        queries[span, :] = (block * inverse * gain[...]).astype(BF16)

    own_hidden[...] = hidden[pl.ds(pl.multiple_of(z * rows, rows), rows), :]
    for copy in copies:
        copy.wait()

    def score(b):
        span = slice(b * BLOCK, (b + 1) * BLOCK)
        top = None
        for j in range(4):
            product = (
                lax.dot_general(
                    queries[span, :], held[j], (((1,), (1,)), ((), ())), preferred_element_type=F32
                )
                * factor
            )
            scores[span, j * count : (j + 1) * count] = product
            for g in range(count // 128):
                part = product[:, g * 128 : (g + 1) * 128]
                top = part if top is None else jnp.maximum(top, part)
        peaks[span, :] = top

    def soften(b):
        size = 32
        lane = lax.broadcasted_iota(jnp.int32, (size, 128), 1)
        for q in range(BLOCK // size):
            span = slice(b * BLOCK + q * size, b * BLOCK + (q + 1) * size)
            peak = jnp.max(peaks[span, :], axis=1, keepdims=True).astype(BF16).astype(F32)
            ids = wanted[span, 0:1].astype(jnp.int32)
            partial = jnp.zeros((size, 128), F32)
            for j in range(4):
                local = ids - place[3 + j]
                for g in range(count // 128):
                    columns = slice(j * count + g * 128, j * count + (g + 1) * 128)
                    powers = jnp.exp(scores[span, columns] - peak)
                    powers = jnp.where(lane == local - g * 128, 0.0, powers)
                    probs[span, columns] = powers.astype(BF16)
                    partial += powers
            table[span, :] = tail(peak, jnp.sum(partial, axis=1, keepdims=True))

    def gather(b):
        span = slice(b * BLOCK, (b + 1) * BLOCK)
        total = None
        for j in range(4):
            part = jnp.dot(
                probs[span, j * count : (j + 1) * count], held[j], preferred_element_type=F32
            )
            total = part if total is None else total + part
        hidden[span, :] = total

    blocks = RING * rows // BLOCK
    score(0)
    for b in range(blocks):
        if b + 1 < blocks:
            score(b + 1)
        soften(b)
        gather(b)

    for slot, offset in enumerate(REDUCE):
        start = pl.multiple_of(lax.rem(z + offset + RING, RING) * rows, rows)
        outs[slot][:, :width] = hidden[pl.ds(start, rows), :].astype(BF16)
        outs[slot][:, width:] = table[pl.ds(start, rows), :]


def tail(peak, total):
    lane = lax.broadcasted_iota(jnp.int32, (peak.shape[0], 128), 1)
    high = total.astype(BF16).astype(F32)
    columns = jnp.where(lane == 0, peak, jnp.where(lane == 1, high, total - high))
    return jnp.where(lane < 3, columns, 0.0).astype(BF16)


def split(block, width):
    end = block[:, width:].astype(F32)
    return (block[:, :width].astype(F32), end[:, 0:1], end[:, 1:2] + end[:, 2:3])


def join(first, second):
    peak = jnp.maximum(first[1], second[1])
    left, right = jnp.exp(first[1] - peak), jnp.exp(second[1] - peak)
    return (first[0] * left + second[0] * right, peak, first[2] * left + second[2] * right)


def merge_kernel(width, first, second, out):
    sums, peak, total = join(split(first[...], width), split(second[...], width))
    out[:, :width] = sums.astype(BF16)
    out[:, width:] = tail(peak, total)


def final_kernel(factor, first, second, own, hidden, gain, picked, weight, out, loss):
    width = hidden.shape[1]
    merged = join(split(first[...], width), split(second[...], width))
    sums, peak, total = join(merged, split(own[...], width))
    values = hidden[...]
    inverse = lax.rsqrt(jnp.mean(values * values, axis=1, keepdims=True) + 1e-06)
    queries = (values * inverse * gain[...]).astype(BF16).astype(F32)
    positive = picked[...].astype(F32)
    score = jnp.sum(queries * positive, axis=1, keepdims=True) * factor
    top = jnp.maximum(peak, score)
    others = jnp.exp(peak - top)
    whole = total * others + jnp.exp(score - top)
    losses = jnp.broadcast_to(top + jnp.log(whole) - score, (values.shape[0], 128))
    loss[...] = losses.T[:1, :]
    share = others / whole
    grad = (sums * share - positive * (total * share)) * (16.0 * factor)
    scaled = gain[...] * grad
    inner = jnp.sum(scaled * values, axis=1, keepdims=True)
    hidden_grad = (
        inverse * scaled - values * (inverse * inverse * inverse) * inner / width
    ).astype(BF16)
    out[...] = lax.dot_general(
        hidden_grad, weight[...], (((1,), (1,)), ((), ())), preferred_element_type=F32
    ).astype(BF16)


def queue_kernel(shift, keys, fresh, out):
    count = keys.shape[0]
    wanted = lax.broadcasted_iota(jnp.int32, (count, 1), 0) + shift[0]
    pick = lax.broadcasted_iota(jnp.int32, (count, fresh.shape[0]), 1) == wanted
    moved = jnp.dot(pick.astype(F32).astype(BF16), fresh[...], preferred_element_type=F32)
    replaced = (wanted >= 0) & (wanted < fresh.shape[0])
    out[...] = jnp.where(replaced, moved, keys[...].astype(F32)).astype(BF16)


def shards(speech, weight, norm_gain, queue_keys, new_keys, pointer, positives):
    rows, width = speech.shape
    count = queue_keys.shape[0]
    total_rows = RING * rows
    queue_length = count * lax.axis_size("queue")
    queue_index = lax.axis_index("queue")
    mp = lax.axis_index("mp")
    z = (queue_index // 2) % RING
    factor = 2.0 / math.sqrt(width)

    core = queue_index % 2
    far = lax.ppermute(queue_keys, "queue", FAR)
    near = lax.ppermute(queue_keys, "queue", CORE)
    flipped = queue_index ^ (2 * RING)
    bases = [index * count for index in (queue_index, queue_index ^ 1, flipped, flipped ^ 1)]
    place = jnp.stack([z, mp, core] + bases).astype(jnp.int32)

    codes = jnp.stack([positives // 128, positives % 128], axis=1).astype(BF16)
    packed = jnp.concatenate([speech, jnp.pad(codes, ((0, 0), (0, 126)))], axis=1)
    slots = {0: packed}
    up = down = packed
    pieces, shard = [], weight
    for step in range(1, 5):
        shares = [(m ^ step, m ^ (step + 4) if step < 4 else m ^ step) for m in range(8)]
        moves = [
            (shares[m][q % 2] + q * 8, m + q * 8) for q in range(4 * RING) for m in range(8)
        ]
        piece = lax.ppermute(shard, ("queue", "mp"), moves)
        up = lax.ppermute(up, "queue", UP)
        if step < 4:
            down = lax.ppermute(down, "queue", DOWN)
            if step == 2:
                near, up = lax.optimization_barrier((near, up))
            piece, up, down, shard = lax.optimization_barrier((piece, up, down, weight))
            slots[step] = down
        slots[-step] = up
        pieces.append(piece)
    other_pieces = lax.ppermute(jnp.concatenate(pieces[:3], axis=0), "queue", CORE)
    fresh, slots[-4] = lax.optimization_barrier((new_keys, slots[-4]))
    shift = (queue_index * count - pointer) % queue_length
    shift = jnp.where(shift >= queue_length - count, shift - queue_length, shift)
    queue_next = pl.pallas_call(
        queue_kernel,
        out_shape=jax.ShapeDtypeStruct(queue_keys.shape, BF16),
        in_specs=[smem(), vmem(), vmem()],
        out_specs=vmem(),
        compiler_params=limit(12),
        cost_estimate=pl.CostEstimate(
            flops=2 * count * count * width, bytes_accessed=5_000_000, transcendentals=0
        ),
        name="queue",
    )(shift, queue_keys, fresh)
    far, queue_next, pieces[3] = lax.optimization_barrier((far, queue_next, pieces[3]))
    far_near = lax.ppermute(far, "queue", CORE)
    far_near, other_pieces = lax.optimization_barrier((far_near, other_pieces))
    keys = (queue_keys, near, far, far_near)

    gain = norm_gain.reshape(1, width)
    gathered = [slots[offset] for offset in GATHER]

    picked = pl.pallas_call(
        functools.partial(picked_kernel, rows),
        out_shape=jax.ShapeDtypeStruct((total_rows, width), BF16),
        in_specs=[smem()] + [vmem()] * RING + [anywhere()] * 4,
        out_specs=vmem(),
        scratch_shapes=[
            pltpu.VMEM((4, count, width), BF16),
            pltpu.VMEM((total_rows, 128), F32),
            pltpu.VMEM((total_rows, 4 * count), BF16),
            pltpu.SemaphoreType.DMA((4,)),
        ],
        compiler_params=limit(22),
        cost_estimate=pl.CostEstimate(
            flops=2 * total_rows * width * 4 * count, bytes_accessed=10_000_000, transcendentals=0
        ),
        name="picked",
    )(place, *gathered, *keys)
    groups = [
        [(x * RING + k) * 2 + c for k in range(RING)] for x in range(2) for c in range(2)
    ]
    own_picked = lax.psum_scatter(
        picked, "queue", scatter_dimension=0, axis_index_groups=groups, tiled=True
    )

    block = jax.ShapeDtypeStruct((rows, width + 128), BF16)
    *grads, own_hidden, full_weight = pl.pallas_call(
        functools.partial(score_kernel, factor, rows),
        out_shape=[block] * RING
        + [
            jax.ShapeDtypeStruct((rows, width), F32),
            jax.ShapeDtypeStruct((width, width), BF16),
        ],
        in_specs=[smem()] + [vmem()] * (RING + 7) + [anywhere()] * 4,
        out_specs=[vmem()] * (RING + 2),
        scratch_shapes=[
            pltpu.VMEM((total_rows, width), BF16),
            pltpu.VMEM((total_rows, width), F32),
            pltpu.VMEM((total_rows, width), BF16),
            pltpu.VMEM((total_rows, 4 * count), F32),
            pltpu.VMEM((total_rows, 4 * count), BF16),
            pltpu.VMEM((total_rows, 128), F32),
            pltpu.VMEM((total_rows, 128), F32),
            pltpu.VMEM((total_rows, 128), BF16),
            pltpu.VMEM((4, count, width), BF16),
            pltpu.SemaphoreType.DMA((4,)),
        ],
        compiler_params=limit(46),
        cost_estimate=pl.CostEstimate(
            flops=2 * total_rows * width * (8 * count + width),
            bytes_accessed=16_000_000,
            transcendentals=total_rows * 4 * count,
        ),
        name="scores",
    )(place, *gathered, weight, *pieces, other_pieces, gain, *keys)
    grads = dict(zip(REDUCE, grads))

    def merge(first, second):
        return pl.pallas_call(
            functools.partial(merge_kernel, width),
            out_shape=block,
            in_specs=[vmem()] * 2,
            out_specs=vmem(),
            compiler_params=limit(4),
            cost_estimate=pl.CostEstimate(
                flops=4 * rows * width, bytes_accessed=600_000, transcendentals=2 * rows
            ),
            name="merge",
        )(first, second)

    first, second = grads[4], grads[-3]
    for step in range(4):
        first = lax.ppermute(first, "queue", UP)
        if step < 3:
            first = merge(first, grads[3 - step])
            second = lax.ppermute(second, "queue", DOWN)
            if step < 2:
                second = merge(second, grads[step - 2])

    grad_speech, losses = pl.pallas_call(
        functools.partial(final_kernel, factor),
        out_shape=(
            jax.ShapeDtypeStruct((rows, width), BF16),
            jax.ShapeDtypeStruct((1, rows), F32),
        ),
        in_specs=[vmem()] * 7,
        out_specs=(vmem(),) * 2,
        compiler_params=limit(8),
        cost_estimate=pl.CostEstimate(
            flops=2 * rows * width * width, bytes_accessed=3_500_000, transcendentals=rows
        ),
        name="final",
    )(first, second, grads[0], own_hidden, gain, own_picked, full_weight)

    return (losses.reshape(rows), grad_speech, queue_next)


def solution(mesh):
    return jax.shard_map(
        shards,
        mesh=mesh,
        in_specs=(
            P(("queue", "mp"), None),
            P(None, "mp"),
            P(),
            P("queue", None),
            P(),
            P(),
            P(("queue", "mp")),
        ),
        out_specs=(P(("queue", "mp")), P(("queue", "mp"), None), P("queue", None)),
        check_vma=False,
    )
```

```python
import functools
import math

import jax
import jax.numpy as jnp
from jax import lax
from jax.experimental import pallas as pl
from jax.experimental.pallas import tpu as pltpu
from jax.sharding import PartitionSpec as P

RING = 8
BLOCK = 256
F32 = jnp.float32
BF16 = jnp.bfloat16
GATHER = (0, -1, 1, -2, 2, -3, 3, -4)
REDUCE = (4, -3, 3, -2, 2, -1, 1, 0)


def limit(mib):
    return pltpu.CompilerParams(vmem_limit_bytes=mib * 1024 * 1024)


def vmem():
    return pl.BlockSpec(memory_space=pltpu.VMEM)


def hbm():
    return pl.BlockSpec(memory_space=pltpu.HBM)


def smem():
    return pl.BlockSpec(memory_space=pltpu.SMEM)


def queue_perm(move):
    def index(x, z, c):
        return (x * RING + z) * 2 + c

    return [
        (index(x, z, c), index(*move(x, z, c)))
        for x in range(2)
        for z in range(RING)
        for c in range(2)
    ]


UP = queue_perm(lambda x, z, c: (x, (z + 1) % RING, c))
DOWN = queue_perm(lambda x, z, c: (x, (z - 1) % RING, c))
CORE = queue_perm(lambda x, z, c: (x, z, 1 - c))


def start_all(pairs, sems):
    copies = [
        pltpu.make_async_copy(source, target, sems.at[i])
        for i, (source, target) in enumerate(pairs)
    ]
    for copy in copies:
        copy.start()
    return copies


def slot_spans(rows, z):
    return [
        pl.ds(pl.multiple_of(lax.rem(z + offset + RING, RING) * rows, rows), rows)
        for offset in GATHER
    ]


def unpack_ids(codes, wanted):
    values = codes[...].astype(F32)
    wanted[...] = jnp.broadcast_to(values[:, 0:1] * 128.0 + values[:, 1:2], wanted.shape)


def picked_kernel(rows, place, *refs):
    slots, keys, out = refs[:RING], refs[RING : RING + 4], refs[RING + 4]
    held, codes, wanted, chosen, sems = refs[RING + 5 :]
    width, count = out.shape[1], held.shape[1]
    spans = slot_spans(rows, place[0])
    pairs = [
        (slot.at[:, pl.ds(width, 128)], codes.at[span, :]) for slot, span in zip(slots, spans)
    ]
    copies = start_all(pairs + [(source, held.at[j]) for j, source in enumerate(keys)], sems)
    for copy in copies[:RING]:
        copy.wait()
    copies = copies[RING:]
    unpack_ids(codes, wanted)
    lane = lax.broadcasted_iota(jnp.int32, (BLOCK, 128), 1)
    for b in range(RING * rows // BLOCK):
        span = slice(b * BLOCK, (b + 1) * BLOCK)
        ids = wanted[span, 0:1].astype(jnp.int32)
        total = None
        for j in range(4):
            local = ids - place[3 + j]
            for g in range(count // 128):
                mine = lane == local - g * 128
                start = j * count + g * 128
                chosen[span, start : start + 128] = mine.astype(F32).astype(BF16)
            if b == 0:
                copies[j].wait()
            part = jnp.dot(
                chosen[span, j * count : (j + 1) * count], held[j], preferred_element_type=F32
            )
            total = part if total is None else total + part
        out[span, :] = total.astype(BF16)


def score_kernel(factor, rows, place, *refs):
    slots = refs[:RING]
    own_weight, near_weight = refs[RING], refs[RING + 1 : RING + 6]
    keys, gain = refs[RING + 6 : RING + 10], refs[RING + 10]
    outs = refs[RING + 11 : 2 * RING + 11]
    own_hidden, full_weight = refs[2 * RING + 11 : 2 * RING + 13]
    speech, hidden, queries, scores, probs, codes, wanted, peaks, table, held, sems = refs[
        2 * RING + 13 :
    ]
    z, mp, core = place[0], place[1], place[2]
    width = hidden.shape[1]
    count = held.shape[1]
    piece = own_weight.shape[1]
    spans = slot_spans(rows, z)

    def column(step):
        start = pl.multiple_of(jnp.bitwise_xor(mp, step) * piece, piece)
        return full_weight.at[:, pl.ds(start, piece)]

    pairs = []
    for slot, span in zip(slots, spans):
        pairs.append((slot.at[:, pl.ds(0, width)], speech.at[span, :]))
        pairs.append((slot.at[:, pl.ds(width, 128)], codes.at[span, :]))
    pairs += [(own_weight, column(0)), (near_weight[3], column(4))]
    for i in range(3):
        pairs.append((near_weight[i], column(i + 1 + 4 * core)))
        pairs.append((near_weight[4].at[pl.ds(i * width, width), :], column(i + 5 - 4 * core)))
    first = len(pairs)
    pairs += [(source, held.at[j]) for j, source in enumerate(keys)]
    copies = start_all(pairs, sems)
    for copy in copies[:first]:
        copy.wait()
    unpack_ids(codes, wanted)

    hidden[...] = jnp.dot(speech[...], full_weight[...], preferred_element_type=F32)

    @pl.loop(0, RING)
    def _(b):
        span = pl.ds(pl.multiple_of(b * rows, rows), rows)
        block = hidden[span, :]
        inverse = lax.rsqrt(jnp.mean(block * block, axis=1, keepdims=True) + 1e-06)
        queries[span, :] = (block * inverse * gain[...]).astype(BF16)

    own_hidden[...] = hidden[pl.ds(pl.multiple_of(z * rows, rows), rows), :]
    for copy in copies[first:]:
        copy.wait()

    def score(b):
        span = slice(b * BLOCK, (b + 1) * BLOCK)
        top = None
        for j in range(4):
            product = (
                lax.dot_general(
                    queries[span, :], held[j], (((1,), (1,)), ((), ())), preferred_element_type=F32
                )
                * factor
            )
            scores[span, j * count : (j + 1) * count] = product
            for g in range(count // 128):
                part = product[:, g * 128 : (g + 1) * 128]
                top = part if top is None else jnp.maximum(top, part)
        peaks[span, :] = top

    def soften(b):
        size = 32
        lane = lax.broadcasted_iota(jnp.int32, (size, 128), 1)
        for q in range(BLOCK // size):
            span = slice(b * BLOCK + q * size, b * BLOCK + (q + 1) * size)
            peak = jnp.max(peaks[span, :], axis=1, keepdims=True).astype(BF16).astype(F32)
            ids = wanted[span, 0:1].astype(jnp.int32)
            partial = jnp.zeros((size, 128), F32)
            for j in range(4):
                local = ids - place[3 + j]
                for g in range(count // 128):
                    columns = slice(j * count + g * 128, j * count + (g + 1) * 128)
                    powers = jnp.exp(scores[span, columns] - peak)
                    powers = jnp.where(lane == local - g * 128, 0.0, powers)
                    probs[span, columns] = powers.astype(BF16)
                    partial += powers
            table[span, :] = tail(peak, jnp.sum(partial, axis=1, keepdims=True))

    def gather(b):
        span = slice(b * BLOCK, (b + 1) * BLOCK)
        total = None
        for j in range(4):
            part = jnp.dot(
                probs[span, j * count : (j + 1) * count], held[j], preferred_element_type=F32
            )
            total = part if total is None else total + part
        hidden[span, :] = total

    blocks = RING * rows // BLOCK
    score(0)
    for b in range(blocks):
        if b + 1 < blocks:
            score(b + 1)
        soften(b)
        gather(b)

    for slot, offset in enumerate(REDUCE):
        start = pl.multiple_of(lax.rem(z + offset + RING, RING) * rows, rows)
        outs[slot][:, :width] = hidden[pl.ds(start, rows), :].astype(BF16)
        outs[slot][:, width:] = table[pl.ds(start, rows), :]


def tail(peak, total):
    lane = lax.broadcasted_iota(jnp.int32, (peak.shape[0], 128), 1)
    high = total.astype(BF16).astype(F32)
    columns = jnp.where(lane == 0, peak, jnp.where(lane == 1, high, total - high))
    return jnp.where(lane < 3, columns, 0.0).astype(BF16)


def split(block, width):
    end = block[:, width:].astype(F32)
    return (block[:, :width].astype(F32), end[:, 0:1], end[:, 1:2] + end[:, 2:3])


def join(first, second):
    peak = jnp.maximum(first[1], second[1])
    left, right = jnp.exp(first[1] - peak), jnp.exp(second[1] - peak)
    return (first[0] * left + second[0] * right, peak, first[2] * left + second[2] * right)


def merge_kernel(width, first, second, out):
    sums, peak, total = join(split(first[...], width), split(second[...], width))
    out[:, :width] = sums.astype(BF16)
    out[:, width:] = tail(peak, total)


def final_kernel(factor, first, second, own, hidden, gain, picked, weight, out, loss):
    width = hidden.shape[1]
    merged = join(split(first[...], width), split(second[...], width))
    sums, peak, total = join(merged, split(own[...], width))
    values = hidden[...]
    inverse = lax.rsqrt(jnp.mean(values * values, axis=1, keepdims=True) + 1e-06)
    queries = (values * inverse * gain[...]).astype(BF16).astype(F32)
    positive = picked[...].astype(F32)
    score = jnp.sum(queries * positive, axis=1, keepdims=True) * factor
    top = jnp.maximum(peak, score)
    others = jnp.exp(peak - top)
    whole = total * others + jnp.exp(score - top)
    losses = jnp.broadcast_to(top + jnp.log(whole) - score, (values.shape[0], 128))
    loss[...] = losses.T[:1, :]
    share = others / whole
    grad = (sums * share - positive * (total * share)) * (16.0 * factor)
    scaled = gain[...] * grad
    inner = jnp.sum(scaled * values, axis=1, keepdims=True)
    hidden_grad = (
        inverse * scaled - values * (inverse * inverse * inverse) * inner / width
    ).astype(BF16)
    out[...] = lax.dot_general(
        hidden_grad, weight[...], (((1,), (1,)), ((), ())), preferred_element_type=F32
    ).astype(BF16)


def queue_kernel(shift, keys, fresh, out):
    count = keys.shape[0]
    wanted = lax.broadcasted_iota(jnp.int32, (count, 1), 0) + shift[0]
    pick = lax.broadcasted_iota(jnp.int32, (count, fresh.shape[0]), 1) == wanted
    moved = jnp.dot(pick.astype(F32).astype(BF16), fresh[...], preferred_element_type=F32)
    replaced = (wanted >= 0) & (wanted < fresh.shape[0])
    out[...] = jnp.where(replaced, moved, keys[...].astype(F32)).astype(BF16)


def shards(speech, weight, norm_gain, queue_keys, new_keys, pointer, positives):
    rows, width = speech.shape
    count = queue_keys.shape[0]
    total_rows = RING * rows
    queue_length = count * lax.axis_size("queue")
    queue_index = lax.axis_index("queue")
    mp = lax.axis_index("mp")
    z = (queue_index // 2) % RING
    factor = 2.0 / math.sqrt(width)

    core = queue_index % 2
    half = RING * 2
    across = [
        (q * 8 + m, (q ^ half) * 8 + (m ^ 4)) for q in range(4 * RING) for m in range(8)
    ]
    far = lax.ppermute(queue_keys, ("queue", "mp"), across)
    near = lax.ppermute(queue_keys, "queue", CORE)
    flipped = queue_index ^ (2 * RING)
    bases = [index * count for index in (queue_index, queue_index ^ 1, flipped, flipped ^ 1)]
    place = jnp.stack([z, mp, core] + bases).astype(jnp.int32)

    codes = jnp.stack([positives // 128, positives % 128], axis=1).astype(BF16)
    packed = jnp.concatenate([speech, jnp.pad(codes, ((0, 0), (0, 126)))], axis=1)
    slots = {0: packed}
    up = down = packed
    pieces, shard = [], weight
    for step in range(1, 5):
        shares = [(m ^ step, m ^ (step + 4) if step < 4 else m ^ step) for m in range(8)]
        moves = [
            (shares[m][q % 2] + q * 8, m + q * 8) for q in range(4 * RING) for m in range(8)
        ]
        piece = lax.ppermute(shard, ("queue", "mp"), moves)
        up = lax.ppermute(up, "queue", UP)
        if step < 4:
            down = lax.ppermute(down, "queue", DOWN)
            if step == 2:
                near, up = lax.optimization_barrier((near, up))
            piece, up, down, shard = lax.optimization_barrier((piece, up, down, weight))
            slots[step] = down
        slots[-step] = up
        pieces.append(piece)
    other_pieces = lax.ppermute(jnp.concatenate(pieces[:3], axis=0), "queue", CORE)
    fresh, slots[-4] = lax.optimization_barrier((new_keys, slots[-4]))
    shift = (queue_index * count - pointer) % queue_length
    shift = jnp.where(shift >= queue_length - count, shift - queue_length, shift)
    queue_next = pl.pallas_call(
        queue_kernel,
        out_shape=jax.ShapeDtypeStruct(queue_keys.shape, BF16),
        in_specs=[smem(), vmem(), vmem()],
        out_specs=vmem(),
        compiler_params=limit(50),
        cost_estimate=pl.CostEstimate(
            flops=2 * count * count * width, bytes_accessed=5_000_000, transcendentals=0
        ),
        name="queue",
    )(shift, queue_keys, fresh)
    far, queue_next, pieces[3] = lax.optimization_barrier((far, queue_next, pieces[3]))
    far_near = lax.ppermute(far, "queue", CORE)
    far_near, other_pieces = lax.optimization_barrier((far_near, other_pieces))
    keys = (queue_keys, near, far, far_near)

    gain = norm_gain.reshape(1, width)
    gathered = [slots[offset] for offset in GATHER]

    picked = pl.pallas_call(
        functools.partial(picked_kernel, rows),
        out_shape=jax.ShapeDtypeStruct((total_rows, width), BF16),
        in_specs=[smem()] + [hbm()] * (RING + 4),
        out_specs=vmem(),
        scratch_shapes=[
            pltpu.VMEM((4, count, width), BF16),
            pltpu.VMEM((total_rows, 128), BF16),
            pltpu.VMEM((total_rows, 128), F32),
            pltpu.VMEM((total_rows, 4 * count), BF16),
            pltpu.SemaphoreType.DMA((RING + 4,)),
        ],
        compiler_params=limit(50),
        cost_estimate=pl.CostEstimate(
            flops=2 * total_rows * width * 4 * count, bytes_accessed=10_000_000, transcendentals=0
        ),
        name="picked",
    )(place, *gathered, *keys)
    groups = [
        [(x * RING + k) * 2 + c for k in range(RING)] for x in range(2) for c in range(2)
    ]
    own_picked = lax.psum_scatter(
        picked, "queue", scatter_dimension=0, axis_index_groups=groups, tiled=True
    )

    block = jax.ShapeDtypeStruct((rows, width + 128), BF16)
    *grads, own_hidden, full_weight = pl.pallas_call(
        functools.partial(score_kernel, factor, rows),
        out_shape=[block] * RING
        + [
            jax.ShapeDtypeStruct((rows, width), F32),
            jax.ShapeDtypeStruct((width, width), BF16),
        ],
        in_specs=[smem()] + [hbm()] * (RING + 10) + [vmem()],
        out_specs=[vmem()] * (RING + 2),
        scratch_shapes=[
            pltpu.VMEM((total_rows, width), BF16),
            pltpu.VMEM((total_rows, width), F32),
            pltpu.VMEM((total_rows, width), BF16),
            pltpu.VMEM((total_rows, 4 * count), F32),
            pltpu.VMEM((total_rows, 4 * count), BF16),
            pltpu.VMEM((total_rows, 128), BF16),
            pltpu.VMEM((total_rows, 128), F32),
            pltpu.VMEM((total_rows, 128), F32),
            pltpu.VMEM((total_rows, 128), BF16),
            pltpu.VMEM((4, count, width), BF16),
            pltpu.SemaphoreType.DMA((2 * RING + 12,)),
        ],
        compiler_params=limit(50),
        cost_estimate=pl.CostEstimate(
            flops=2 * total_rows * width * (8 * count + width),
            bytes_accessed=16_000_000,
            transcendentals=total_rows * 4 * count,
        ),
        name="scores",
    )(place, *gathered, weight, *pieces, other_pieces, *keys, gain)
    grads = dict(zip(REDUCE, grads))

    def merge(first, second):
        return pl.pallas_call(
            functools.partial(merge_kernel, width),
            out_shape=block,
            in_specs=[vmem()] * 2,
            out_specs=vmem(),
            compiler_params=limit(4),
            cost_estimate=pl.CostEstimate(
                flops=4 * rows * width, bytes_accessed=600_000, transcendentals=2 * rows
            ),
            name="merge",
        )(first, second)

    first, second = grads[4], grads[-3]
    for step in range(4):
        first = lax.ppermute(first, "queue", UP)
        if step < 3:
            first = merge(first, grads[3 - step])
            second = lax.ppermute(second, "queue", DOWN)
            if step < 2:
                second = merge(second, grads[step - 2])

    grad_speech, losses = pl.pallas_call(
        functools.partial(final_kernel, factor),
        out_shape=(
            jax.ShapeDtypeStruct((rows, width), BF16),
            jax.ShapeDtypeStruct((1, rows), F32),
        ),
        in_specs=[vmem()] * 7,
        out_specs=(vmem(),) * 2,
        compiler_params=limit(8),
        cost_estimate=pl.CostEstimate(
            flops=2 * rows * width * width, bytes_accessed=3_500_000, transcendentals=rows
        ),
        name="final",
    )(first, second, grads[0], own_hidden, gain, own_picked, full_weight)

    return (losses.reshape(rows), grad_speech, queue_next)


def solution(mesh):
    return jax.shard_map(
        shards,
        mesh=mesh,
        in_specs=(
            P(("queue", "mp"), None),
            P(None, "mp"),
            P(),
            P("queue", None),
            P(),
            P(),
            P(("queue", "mp")),
        ),
        out_specs=(P(("queue", "mp")), P(("queue", "mp"), None), P("queue", None)),
        check_vma=False,
    )
```

```python
import functools
import math

import jax
import jax.numpy as jnp
from jax import lax
from jax.experimental import pallas as pl
from jax.experimental.pallas import tpu as pltpu
from jax.sharding import PartitionSpec as P

RING = 8
BLOCK = 256
F32 = jnp.float32
BF16 = jnp.bfloat16
GATHER = (0, -1, 1, -2, 2, -3, 3, -4)
REDUCE = (4, -3, 3, -2, 2, -1, 1, 0)


def limit(mib):
    return pltpu.CompilerParams(vmem_limit_bytes=mib * 1024 * 1024)


def vmem():
    return pl.BlockSpec(memory_space=pltpu.VMEM)


def hbm():
    return pl.BlockSpec(memory_space=pltpu.HBM)


def smem():
    return pl.BlockSpec(memory_space=pltpu.SMEM)


def queue_perm(move):
    def index(x, z, c):
        return (x * RING + z) * 2 + c

    return [
        (index(x, z, c), index(*move(x, z, c)))
        for x in range(2)
        for z in range(RING)
        for c in range(2)
    ]


UP = queue_perm(lambda x, z, c: (x, (z + 1) % RING, c))
DOWN = queue_perm(lambda x, z, c: (x, (z - 1) % RING, c))
CORE = queue_perm(lambda x, z, c: (x, z, 1 - c))


def start_all(pairs, sems):
    copies = [
        pltpu.make_async_copy(source, target, sems.at[i])
        for i, (source, target) in enumerate(pairs)
    ]
    for copy in copies:
        copy.start()
    return copies


def slot_spans(rows, z):
    return [
        pl.ds(pl.multiple_of(lax.rem(z + offset + RING, RING) * rows, rows), rows)
        for offset in GATHER
    ]


def unpack_ids(codes, wanted):
    values = codes[...].astype(F32)
    wanted[...] = jnp.broadcast_to(values[:, 0:1] * 128.0 + values[:, 1:2], wanted.shape)


def key_pairs(keys, held):
    pairs, start = [], 0
    for source in keys:
        pairs.append((source, held.at[pl.ds(start, source.shape[0]), :]))
        start += source.shape[0]
    return pairs


def picked_kernel(rows, first, place, *refs):
    slots, keys, out = refs[:RING], refs[RING:-6], refs[-6]
    held, codes, wanted, chosen, sems = refs[-5:]
    width, count = out.shape[1], held.shape[0] // 2
    spans = slot_spans(rows, place[0])
    pairs = [
        (slot.at[:, pl.ds(width, 128)], codes.at[span, :]) for slot, span in zip(slots, spans)
    ]
    copies = start_all(pairs + key_pairs(keys, held), sems)
    for copy in copies[:RING]:
        copy.wait()
    copies = copies[RING:]
    unpack_ids(codes, wanted)
    lane = lax.broadcasted_iota(jnp.int32, (BLOCK, 128), 1)
    for b in range(RING * rows // BLOCK):
        span = slice(b * BLOCK, (b + 1) * BLOCK)
        ids = wanted[span, 0:1].astype(jnp.int32)
        total = None
        for j in range(2):
            local = ids - place[3 + first + j]
            for g in range(count // 128):
                mine = lane == local - g * 128
                start = j * count + g * 128
                chosen[span, start : start + 128] = mine.astype(F32).astype(BF16)
            if b == 0:
                share = len(keys) // 2
                for copy in copies[j * share : (j + 1) * share]:
                    copy.wait()
            block = slice(j * count, (j + 1) * count)
            part = jnp.dot(chosen[span, block], held[block, :], preferred_element_type=F32)
            total = part if total is None else total + part
        out[span, :] = total.astype(BF16)


def score_kernel(factor, rows, place, *refs):
    slots = refs[:RING]
    own_weight, near_weight = refs[RING], refs[RING + 1 : RING + 6]
    keys, gain = refs[RING + 6 : RING + 12], refs[RING + 12]
    sums, stats, own_hidden, full_weight = refs[RING + 13 : RING + 17]
    speech, hidden, queries, scores, probs, codes, wanted, peaks, table, held, sems = refs[
        RING + 17 :
    ]
    z, mp, core = place[0], place[1], place[2]
    width = hidden.shape[1]
    count = held.shape[0] // 4
    piece = own_weight.shape[1]
    spans = slot_spans(rows, z)

    def column(step):
        start = pl.multiple_of(jnp.bitwise_xor(mp, step) * piece, piece)
        return full_weight.at[:, pl.ds(start, piece)]

    pairs = []
    for slot, span in zip(slots, spans):
        pairs.append((slot.at[:, pl.ds(0, width)], speech.at[span, :]))
        pairs.append((slot.at[:, pl.ds(width, 128)], codes.at[span, :]))
    pairs += [(own_weight, column(0)), (near_weight[3], column(4))]
    for i in range(3):
        pairs.append((near_weight[i], column(i + 1 + 4 * core)))
        pairs.append((near_weight[4].at[pl.ds(i * width, width), :], column(i + 5 - 4 * core)))
    first = len(pairs)
    pairs += key_pairs(keys, held)
    copies = start_all(pairs, sems)
    for copy in copies[:first]:
        copy.wait()
    unpack_ids(codes, wanted)

    hidden[...] = jnp.dot(speech[...], full_weight[...], preferred_element_type=F32)

    @pl.loop(0, RING)
    def _(b):
        span = pl.ds(pl.multiple_of(b * rows, rows), rows)
        block = hidden[span, :]
        inverse = lax.rsqrt(jnp.mean(block * block, axis=1, keepdims=True) + 1e-06)
        queries[span, :] = (block * inverse * gain[...]).astype(BF16)

    own_hidden[...] = hidden[pl.ds(pl.multiple_of(z * rows, rows), rows), :]
    for copy in copies[first:]:
        copy.wait()

    def score(b):
        span = slice(b * BLOCK, (b + 1) * BLOCK)
        top = None
        for j in range(4):
            product = (
                lax.dot_general(
                    queries[span, :],
                    held[j * count : (j + 1) * count, :],
                    (((1,), (1,)), ((), ())),
                    preferred_element_type=F32,
                )
                * factor
            )
            scores[span, j * count : (j + 1) * count] = product
            for g in range(count // 128):
                part = product[:, g * 128 : (g + 1) * 128]
                top = part if top is None else jnp.maximum(top, part)
        peaks[span, :] = top

    def soften(b):
        size = 32
        lane = lax.broadcasted_iota(jnp.int32, (size, 128), 1)
        for q in range(BLOCK // size):
            span = slice(b * BLOCK + q * size, b * BLOCK + (q + 1) * size)
            peak = jnp.max(peaks[span, :], axis=1, keepdims=True)
            ids = wanted[span, 0:1].astype(jnp.int32)
            partial = jnp.zeros((size, 128), F32)
            found = jnp.zeros((size, 128), F32)
            for j in range(4):
                local = ids - place[3 + j]
                for g in range(count // 128):
                    columns = slice(j * count + g * 128, j * count + (g + 1) * 128)
                    values = scores[span, columns]
                    powers = jnp.exp(values - peak)
                    probs[span, columns] = powers.astype(BF16)
                    partial += powers
                    found += jnp.where(lane == local - g * 128, values, 0.0)
            total = jnp.sum(partial, axis=1, keepdims=True)
            score_here = jnp.sum(found, axis=1, keepdims=True)
            table[span, :] = jnp.where(
                lane == 0, peak, jnp.where(lane == 1, total, score_here)
            )

    def gather(b):
        span = slice(b * BLOCK, (b + 1) * BLOCK)
        total = None
        for j in range(4):
            block = slice(j * count, (j + 1) * count)
            part = jnp.dot(probs[span, block], held[block, :], preferred_element_type=F32)
            total = part if total is None else total + part
        sums[span, :] = total

    blocks = RING * rows // BLOCK
    score(0)
    for b in range(blocks):
        if b + 1 < blocks:
            score(b + 1)
        soften(b)
        gather(b)
    stats[...] = table[...].T[:8, :]


def join_kernel(count, *refs):
    parts, out = refs[:count], refs[count]
    peak = parts[0][0:1, :]
    for part in parts[1:]:
        peak = jnp.maximum(peak, part[0:1, :])
    total = found = 0.0
    for part in parts:
        total += part[1:2, :] * jnp.exp(part[0:1, :] - peak)
        found += part[2:3, :]
    row = lax.broadcasted_iota(jnp.int32, out.shape, 0)
    out[...] = jnp.where(row == 0, peak, jnp.where(row == 1, total, found))


def scale_kernel(rows, place, sums, near_picked, far_picked, local, merged, *refs):
    outs, loss, table = refs[:RING], refs[RING], refs[RING + 1]
    log_total = merged[0:1, :] + jnp.log(merged[1:2, :])
    scale = jnp.exp(local[0:1, :] - log_total)
    losses = log_total - merged[2:3, :]
    row = lax.broadcasted_iota(jnp.int32, (128, scale.shape[1]), 0)
    table[...] = jnp.where(row == 0, scale, losses).T

    def span_of(offset):
        start = lax.rem(place[0] + offset + RING, RING) * rows
        return pl.ds(pl.multiple_of(start, rows), rows)

    for slot, offset in enumerate(REDUCE):
        span = span_of(offset)
        picked = near_picked[span, :].astype(F32) + far_picked[span, :].astype(F32)
        outs[slot][...] = (table[span, 0:1] * sums[span, :] - picked).astype(BF16)
    own = jnp.broadcast_to(table[span_of(0), 1:2], (rows, 128))
    loss[...] = own.T[:1, :]


def add_kernel(first, second, out):
    out[...] = (first[...].astype(F32) + second[...].astype(F32)).astype(BF16)


def final_kernel(factor, first, second, own, hidden, gain, weight, out):
    width = hidden.shape[1]
    grad = (first[...].astype(F32) + second[...].astype(F32) + own[...].astype(F32)) * factor
    scaled = gain[...] * grad
    values = hidden[...]
    inverse = lax.rsqrt(jnp.mean(values * values, axis=1, keepdims=True) + 1e-06)
    inner = jnp.sum(scaled * values, axis=1, keepdims=True)
    hidden_grad = (
        inverse * scaled - values * (inverse * inverse * inverse) * inner / width
    ).astype(BF16)
    out[...] = lax.dot_general(
        hidden_grad, weight[...], (((1,), (1,)), ((), ())), preferred_element_type=F32
    ).astype(BF16)


def queue_kernel(shift, keys, fresh, out):
    count = keys.shape[0]
    wanted = lax.broadcasted_iota(jnp.int32, (count, 1), 0) + shift[0]
    pick = lax.broadcasted_iota(jnp.int32, (count, fresh.shape[0]), 1) == wanted
    moved = jnp.dot(pick.astype(F32).astype(BF16), fresh[...], preferred_element_type=F32)
    replaced = (wanted >= 0) & (wanted < fresh.shape[0])
    out[...] = jnp.where(replaced, moved, keys[...].astype(F32)).astype(BF16)


def shards(speech, weight, norm_gain, queue_keys, new_keys, pointer, positives):
    rows, width = speech.shape
    count = queue_keys.shape[0]
    total_rows = RING * rows
    queue_length = count * lax.axis_size("queue")
    queue_index = lax.axis_index("queue")
    mp = lax.axis_index("mp")
    z = (queue_index // 2) % RING
    factor = 2.0 / math.sqrt(width)

    core = queue_index % 2
    half = RING * 2
    across = [
        (q * 8 + m, (q ^ half) * 8 + (m ^ 4)) for q in range(4 * RING) for m in range(8)
    ]
    part = count // 2
    far_first = lax.ppermute(queue_keys[:part], ("queue", "mp"), across)
    far_last = lax.ppermute(queue_keys[part:], ("queue", "mp"), across)
    near = lax.ppermute(queue_keys, "queue", CORE)
    flipped = queue_index ^ (2 * RING)
    bases = [index * count for index in (queue_index, queue_index ^ 1, flipped, flipped ^ 1)]
    place = jnp.stack([z, mp, core] + bases).astype(jnp.int32)

    codes = jnp.stack([positives // 128, positives % 128], axis=1).astype(BF16)
    packed = jnp.concatenate([speech, jnp.pad(codes, ((0, 0), (0, 126)))], axis=1)
    slots = {0: packed}
    up = down = packed
    pieces, shard = [], weight
    for step in range(1, 5):
        shares = [(m ^ step, m ^ (step + 4) if step < 4 else m ^ step) for m in range(8)]
        moves = [
            (shares[m][q % 2] + q * 8, m + q * 8) for q in range(4 * RING) for m in range(8)
        ]
        piece = lax.ppermute(shard, ("queue", "mp"), moves)
        up = lax.ppermute(up, "queue", UP)
        if step < 4:
            down = lax.ppermute(down, "queue", DOWN)
            if step == 2:
                near, up = lax.optimization_barrier((near, up))
            piece, up, down, shard = lax.optimization_barrier((piece, up, down, weight))
            if step == 2:
                far_first, up, shard = lax.optimization_barrier((far_first, up, shard))
            if step == 3:
                far_last, up, shard = lax.optimization_barrier((far_last, up, shard))
            slots[step] = down
        slots[-step] = up
        pieces.append(piece)
        if step == 3:
            other_pieces = lax.ppermute(jnp.concatenate(pieces, axis=0), "queue", CORE)
    gathered = [slots[offset] for offset in GATHER]

    def pick(pair, first, place):
        return pl.pallas_call(
            functools.partial(picked_kernel, rows, first),
            out_shape=jax.ShapeDtypeStruct((total_rows, width), BF16),
            in_specs=[smem()] + [hbm()] * (RING + len(pair)),
            out_specs=vmem(),
            scratch_shapes=[
                pltpu.VMEM((2 * count, width), BF16),
                pltpu.VMEM((total_rows, 128), BF16),
                pltpu.VMEM((total_rows, 128), F32),
                pltpu.VMEM((total_rows, 2 * count), BF16),
                pltpu.SemaphoreType.DMA((RING + len(pair),)),
            ],
            compiler_params=limit(50),
            cost_estimate=pl.CostEstimate(
                flops=first * total_rows * width * count, bytes_accessed=1000, transcendentals=0
            ),
            name="picked",
        )(place, *gathered, *pair)

    near_picked = pick((queue_keys, near), 0, place)
    far_keys = (
        far_first,
        far_last,
        lax.ppermute(far_first, "queue", CORE),
        lax.ppermute(far_last, "queue", CORE),
    )
    place, near_picked = lax.optimization_barrier((place, near_picked))
    gain = norm_gain.reshape(1, width)
    sums, stats, own_hidden, full_weight = pl.pallas_call(
        functools.partial(score_kernel, factor, rows),
        out_shape=(
            jax.ShapeDtypeStruct((total_rows, width), F32),
            jax.ShapeDtypeStruct((8, total_rows), F32),
            jax.ShapeDtypeStruct((rows, width), F32),
            jax.ShapeDtypeStruct((width, width), BF16),
        ),
        in_specs=[smem()] + [hbm()] * (RING + 12) + [vmem()],
        out_specs=(vmem(),) * 4,
        scratch_shapes=[
            pltpu.VMEM((total_rows, width), BF16),
            pltpu.VMEM((total_rows, width), F32),
            pltpu.VMEM((total_rows, width), BF16),
            pltpu.VMEM((total_rows, 4 * count), F32),
            pltpu.VMEM((total_rows, 4 * count), BF16),
            pltpu.VMEM((total_rows, 128), BF16),
            pltpu.VMEM((total_rows, 128), F32),
            pltpu.VMEM((total_rows, 128), F32),
            pltpu.VMEM((total_rows, 128), F32),
            pltpu.VMEM((4 * count, width), BF16),
            pltpu.SemaphoreType.DMA((2 * RING + 14,)),
        ],
        compiler_params=limit(50),
        cost_estimate=pl.CostEstimate(
            flops=2 * total_rows * width * (8 * count + width),
            bytes_accessed=16_000_000,
            transcendentals=total_rows * 4 * count,
        ),
        name="scores",
    )(place, *gathered, weight, *pieces, other_pieces, queue_keys, near, *far_keys, gain)

    def join(*parts):
        return pl.pallas_call(
            functools.partial(join_kernel, len(parts)),
            out_shape=jax.ShapeDtypeStruct(stats.shape, F32),
            in_specs=[vmem()] * len(parts),
            out_specs=vmem(),
            compiler_params=limit(2),
            name="join",
        )(*parts)

    def swap(values, step):
        return lax.ppermute(values, "queue", queue_perm(lambda x, z, c: (x, z ^ step, c)))

    later, stats = lax.optimization_barrier((place, stats))
    other = swap(stats, 1)
    far_picked = pick(far_keys, 2, later)
    other, far_picked = lax.optimization_barrier((other, far_picked))
    pair = join(stats, other)
    merged = join(pair, *[swap(pair, step) for step in (2, 4, 6)])

    *grads, losses = pl.pallas_call(
        functools.partial(scale_kernel, rows),
        out_shape=[jax.ShapeDtypeStruct((rows, width), BF16)] * RING
        + [jax.ShapeDtypeStruct((1, rows), F32)],
        in_specs=[smem()] + [vmem()] * 5,
        out_specs=[vmem()] * (RING + 1),
        scratch_shapes=[pltpu.VMEM((total_rows, 128), F32)],
        compiler_params=limit(16),
        cost_estimate=pl.CostEstimate(
            flops=3 * total_rows * width, bytes_accessed=6_000_000, transcendentals=2000
        ),
        name="scaled",
    )(place, sums, near_picked, far_picked, stats, merged)
    grads = dict(zip(REDUCE, grads))

    def add(first, second):
        return pl.pallas_call(
            add_kernel,
            out_shape=jax.ShapeDtypeStruct((rows, width), BF16),
            in_specs=[vmem()] * 2,
            out_specs=vmem(),
            compiler_params=limit(4),
            cost_estimate=pl.CostEstimate(
                flops=rows * width, bytes_accessed=600_000, transcendentals=0
            ),
            name="add",
        )(first, second)

    shift = (queue_index * count - pointer) % queue_length
    shift = jnp.where(shift >= queue_length - count, shift - queue_length, shift)
    fresh, grads[0] = lax.optimization_barrier((new_keys, grads[0]))
    queue_next = pl.pallas_call(
        queue_kernel,
        out_shape=jax.ShapeDtypeStruct(queue_keys.shape, BF16),
        in_specs=[smem(), vmem(), vmem()],
        out_specs=vmem(),
        compiler_params=limit(12),
        cost_estimate=pl.CostEstimate(
            flops=2 * count * count * width, bytes_accessed=5_000_000, transcendentals=0
        ),
        name="queue",
    )(shift, queue_keys, fresh)

    first, second = grads[4], grads[-3]
    for step in range(4):
        first = lax.ppermute(first, "queue", UP)
        if step == 0:
            first, queue_next = lax.optimization_barrier((first, queue_next))
        if step < 3:
            first = add(first, grads[3 - step])
            second = lax.ppermute(second, "queue", DOWN)
            if step < 2:
                second = add(second, grads[step - 2])

    grad_speech = pl.pallas_call(
        functools.partial(final_kernel, 16.0 * factor),
        out_shape=jax.ShapeDtypeStruct((rows, width), BF16),
        in_specs=[vmem()] * 6,
        out_specs=vmem(),
        compiler_params=limit(8),
        cost_estimate=pl.CostEstimate(
            flops=2 * rows * width * width, bytes_accessed=3_500_000, transcendentals=rows
        ),
        name="final",
    )(first, second, grads[0], own_hidden, gain, full_weight)
    return (losses.reshape(rows), grad_speech, queue_next)


def solution(mesh):
    return jax.shard_map(
        shards,
        mesh=mesh,
        in_specs=(
            P(("queue", "mp"), None),
            P(None, "mp"),
            P(),
            P("queue", None),
            P(),
            P(),
            P(("queue", "mp")),
        ),
        out_specs=(P(("queue", "mp")), P(("queue", "mp"), None), P("queue", None)),
        check_vma=False,
    )
```

```python
import functools
import math

import jax
import jax.numpy as jnp
from jax import lax
from jax.experimental import pallas as pl
from jax.experimental.pallas import tpu as pltpu
from jax.sharding import PartitionSpec as P

RING = 8
BLOCK = 256
F32 = jnp.float32
BF16 = jnp.bfloat16
GATHER = (0, -1, 1, -2, 2, -3, 3, -4)
REDUCE = (4, -3, 3, -2, 2, -1, 1, 0)


def limit(mib):
    return pltpu.CompilerParams(vmem_limit_bytes=mib * 1024 * 1024)


def vmem():
    return pl.BlockSpec(memory_space=pltpu.VMEM)


def hbm():
    return pl.BlockSpec(memory_space=pltpu.HBM)


def smem():
    return pl.BlockSpec(memory_space=pltpu.SMEM)


def queue_perm(move):
    def index(x, z, c):
        return (x * RING + z) * 2 + c

    return [
        (index(x, z, c), index(*move(x, z, c)))
        for x in range(2)
        for z in range(RING)
        for c in range(2)
    ]


UP = queue_perm(lambda x, z, c: (x, (z + 1) % RING, c))
DOWN = queue_perm(lambda x, z, c: (x, (z - 1) % RING, c))
CORE = queue_perm(lambda x, z, c: (x, z, 1 - c))


def start_all(pairs, sems):
    copies = [
        pltpu.make_async_copy(source, target, sems.at[i])
        for i, (source, target) in enumerate(pairs)
    ]
    for copy in copies:
        copy.start()
    return copies


def slot_spans(rows, z):
    return [
        pl.ds(pl.multiple_of(lax.rem(z + offset + RING, RING) * rows, rows), rows)
        for offset in GATHER
    ]


def unpack_ids(codes, wanted):
    values = codes[...].astype(F32)
    wanted[...] = jnp.broadcast_to(values[:, 0:1] * 128.0 + values[:, 1:2], wanted.shape)


def key_pairs(keys, held):
    pairs, start = [], 0
    for source in keys:
        pairs.append((source, held.at[pl.ds(start, source.shape[0]), :]))
        start += source.shape[0]
    return pairs


def picked_kernel(rows, first, place, *refs):
    slots, keys, out = refs[:RING], refs[RING:-6], refs[-6]
    held, codes, wanted, chosen, sems = refs[-5:]
    width, count = out.shape[1], held.shape[0] // 2
    spans = slot_spans(rows, place[0])
    pairs = [
        (slot.at[:, pl.ds(width, 128)], codes.at[span, :]) for slot, span in zip(slots, spans)
    ]
    copies = start_all(pairs + key_pairs(keys, held), sems)
    for copy in copies[:RING]:
        copy.wait()
    copies = copies[RING:]
    unpack_ids(codes, wanted)
    lane = lax.broadcasted_iota(jnp.int32, (BLOCK, 128), 1)
    for b in range(RING * rows // BLOCK):
        span = slice(b * BLOCK, (b + 1) * BLOCK)
        ids = wanted[span, 0:1].astype(jnp.int32)
        total = None
        for j in range(2):
            local = ids - place[3 + first + j]
            for g in range(count // 128):
                mine = lane == local - g * 128
                start = j * count + g * 128
                chosen[span, start : start + 128] = mine.astype(F32).astype(BF16)
            if b == 0:
                share = len(keys) // 2
                for copy in copies[j * share : (j + 1) * share]:
                    copy.wait()
            block = slice(j * count, (j + 1) * count)
            part = jnp.dot(chosen[span, block], held[block, :], preferred_element_type=F32)
            total = part if total is None else total + part
        out[span, :] = total.astype(BF16)


def attend(factor, first, place, queries, wanted, held, scores, probs, peaks, table, keep):
    count = held.shape[0] // 2

    def score(b):
        span = slice(b * BLOCK, (b + 1) * BLOCK)
        top = None
        for j in range(2):
            product = (
                lax.dot_general(
                    queries[span, :],
                    held[j * count : (j + 1) * count, :],
                    (((1,), (1,)), ((), ())),
                    preferred_element_type=F32,
                )
                * factor
            )
            scores[span, j * count : (j + 1) * count] = product
            for g in range(count // 128):
                part = product[:, g * 128 : (g + 1) * 128]
                top = part if top is None else jnp.maximum(top, part)
        peaks[span, :] = top

    def soften(b):
        size = 32
        lane = lax.broadcasted_iota(jnp.int32, (size, 128), 1)
        for q in range(BLOCK // size):
            span = slice(b * BLOCK + q * size, b * BLOCK + (q + 1) * size)
            peak = jnp.max(peaks[span, :], axis=1, keepdims=True)
            ids = wanted[span, 0:1].astype(jnp.int32)
            partial = jnp.zeros((size, 128), F32)
            found = jnp.zeros((size, 128), F32)
            for j in range(2):
                local = ids - place[3 + first + j]
                for g in range(count // 128):
                    columns = slice(j * count + g * 128, j * count + (g + 1) * 128)
                    values = scores[span, columns]
                    powers = jnp.exp(values - peak)
                    probs[span, columns] = powers.astype(BF16)
                    partial += powers
                    found += jnp.where(lane == local - g * 128, values, 0.0)
            total = jnp.sum(partial, axis=1, keepdims=True)
            score_here = jnp.sum(found, axis=1, keepdims=True)
            table[span, :] = jnp.where(
                lane == 0, peak, jnp.where(lane == 1, total, score_here)
            )

    def gather(b):
        span = slice(b * BLOCK, (b + 1) * BLOCK)
        total = None
        for j in range(2):
            block = slice(j * count, (j + 1) * count)
            part = jnp.dot(probs[span, block], held[block, :], preferred_element_type=F32)
            total = part if total is None else total + part
        keep(span, total)

    blocks = queries.shape[0] // BLOCK
    score(0)
    for b in range(blocks):
        if b + 1 < blocks:
            score(b + 1)
        soften(b)
        gather(b)


def near_kernel(factor, rows, place, *refs):
    slots = refs[:RING]
    own_weight, near_weight = refs[RING], refs[RING + 1 : RING + 6]
    keys, gain = refs[RING + 6 : RING + 8], refs[RING + 8]
    sums, table, queries, wanted, own_hidden, full_weight = refs[RING + 9 : RING + 15]
    speech, hidden, scores, probs, codes, peaks, held, sems = refs[RING + 15 :]
    z, mp, core = place[0], place[1], place[2]
    width = hidden.shape[1]
    piece = own_weight.shape[1]
    spans = slot_spans(rows, z)

    def column(step):
        start = pl.multiple_of(jnp.bitwise_xor(mp, step) * piece, piece)
        return full_weight.at[:, pl.ds(start, piece)]

    pairs = []
    for slot, span in zip(slots, spans):
        pairs.append((slot.at[:, pl.ds(0, width)], speech.at[span, :]))
        pairs.append((slot.at[:, pl.ds(width, 128)], codes.at[span, :]))
    pairs += [(own_weight, column(0)), (near_weight[3], column(4))]
    for i in range(3):
        pairs.append((near_weight[i], column(i + 1 + 4 * core)))
        pairs.append((near_weight[4].at[pl.ds(i * width, width), :], column(i + 5 - 4 * core)))
    first = len(pairs)
    copies = start_all(pairs + key_pairs(keys, held), sems)
    for copy in copies[:first]:
        copy.wait()
    unpack_ids(codes, wanted)

    hidden[...] = jnp.dot(speech[...], full_weight[...], preferred_element_type=F32)

    @pl.loop(0, RING)
    def _(b):
        span = pl.ds(pl.multiple_of(b * rows, rows), rows)
        block = hidden[span, :]
        inverse = lax.rsqrt(jnp.mean(block * block, axis=1, keepdims=True) + 1e-06)
        queries[span, :] = (block * inverse * gain[...]).astype(BF16)

    own_hidden[...] = hidden[pl.ds(pl.multiple_of(z * rows, rows), rows), :]
    for copy in copies[first:]:
        copy.wait()

    def keep(span, total):
        sums[span, :] = total

    attend(factor, 0, place, queries, wanted, held, scores, probs, peaks, table, keep)


def far_kernel(factor, place, *refs):
    keys, inputs = refs[:2], refs[2:6]
    sums, stats = refs[6], refs[7]
    scores, probs, peaks, table, held, queries, wanted, before, near_sums, sems = refs[8:]
    holders = (queries, wanted, before, near_sums)
    pairs = list(zip(inputs, holders)) + key_pairs(keys, held)
    for copy in start_all(pairs, sems):
        copy.wait()

    def keep(span, total):
        near, far = before[span, :], table[span, :]
        peak = jnp.maximum(near[:, 0:1], far[:, 0:1])
        left, right = jnp.exp(near[:, 0:1] - peak), jnp.exp(far[:, 0:1] - peak)
        sums[span, :] = near_sums[span, :] * left + total * right
        lane = lax.broadcasted_iota(jnp.int32, near.shape, 1)
        table[span, :] = jnp.where(
            lane == 0, peak, jnp.where(lane == 1, near * left + far * right, near + far)
        )

    attend(factor, 2, place, queries, wanted, held, scores, probs, peaks, table, keep)
    stats[...] = table[...].T[:8, :]


def join_kernel(count, *refs):
    parts, out = refs[:count], refs[count]
    peak = parts[0][0:1, :]
    for part in parts[1:]:
        peak = jnp.maximum(peak, part[0:1, :])
    total = found = 0.0
    for part in parts:
        total += part[1:2, :] * jnp.exp(part[0:1, :] - peak)
        found += part[2:3, :]
    row = lax.broadcasted_iota(jnp.int32, out.shape, 0)
    out[...] = jnp.where(row == 0, peak, jnp.where(row == 1, total, found))


def scale_kernel(rows, place, sums, near_picked, far_picked, local, merged, *refs):
    outs, loss, table = refs[:RING], refs[RING], refs[RING + 1]
    log_total = merged[0:1, :] + jnp.log(merged[1:2, :])
    scale = jnp.exp(local[0:1, :] - log_total)
    losses = log_total - merged[2:3, :]
    row = lax.broadcasted_iota(jnp.int32, (128, scale.shape[1]), 0)
    table[...] = jnp.where(row == 0, scale, losses).T

    def span_of(offset):
        start = lax.rem(place[0] + offset + RING, RING) * rows
        return pl.ds(pl.multiple_of(start, rows), rows)

    for slot, offset in enumerate(REDUCE):
        span = span_of(offset)
        picked = near_picked[span, :].astype(F32) + far_picked[span, :].astype(F32)
        outs[slot][...] = (table[span, 0:1] * sums[span, :] - picked).astype(BF16)
    own = jnp.broadcast_to(table[span_of(0), 1:2], (rows, 128))
    loss[...] = own.T[:1, :]


def add_kernel(first, second, out):
    out[...] = (first[...].astype(F32) + second[...].astype(F32)).astype(BF16)


def final_kernel(factor, first, second, own, hidden, gain, weight, out):
    width = hidden.shape[1]
    grad = (first[...].astype(F32) + second[...].astype(F32) + own[...].astype(F32)) * factor
    scaled = gain[...] * grad
    values = hidden[...]
    inverse = lax.rsqrt(jnp.mean(values * values, axis=1, keepdims=True) + 1e-06)
    inner = jnp.sum(scaled * values, axis=1, keepdims=True)
    hidden_grad = (
        inverse * scaled - values * (inverse * inverse * inverse) * inner / width
    ).astype(BF16)
    out[...] = lax.dot_general(
        hidden_grad, weight[...], (((1,), (1,)), ((), ())), preferred_element_type=F32
    ).astype(BF16)


def queue_kernel(shift, keys, fresh, out):
    count = keys.shape[0]
    wanted = lax.broadcasted_iota(jnp.int32, (count, 1), 0) + shift[0]
    pick = lax.broadcasted_iota(jnp.int32, (count, fresh.shape[0]), 1) == wanted
    moved = jnp.dot(pick.astype(F32).astype(BF16), fresh[...], preferred_element_type=F32)
    replaced = (wanted >= 0) & (wanted < fresh.shape[0])
    out[...] = jnp.where(replaced, moved, keys[...].astype(F32)).astype(BF16)


def shards(speech, weight, norm_gain, queue_keys, new_keys, pointer, positives):
    rows, width = speech.shape
    count = queue_keys.shape[0]
    total_rows = RING * rows
    queue_length = count * lax.axis_size("queue")
    queue_index = lax.axis_index("queue")
    mp = lax.axis_index("mp")
    z = (queue_index // 2) % RING
    factor = 2.0 / math.sqrt(width)

    core = queue_index % 2
    half = RING * 2
    across = [
        (q * 8 + m, (q ^ half) * 8 + (m ^ 4)) for q in range(4 * RING) for m in range(8)
    ]
    far = lax.ppermute(queue_keys, ("queue", "mp"), across)
    near = lax.ppermute(queue_keys, "queue", CORE)
    flipped = queue_index ^ (2 * RING)
    bases = [index * count for index in (queue_index, queue_index ^ 1, flipped, flipped ^ 1)]
    place = jnp.stack([z, mp, core] + bases).astype(jnp.int32)

    codes = jnp.stack([positives // 128, positives % 128], axis=1).astype(BF16)
    packed = jnp.concatenate([speech, jnp.pad(codes, ((0, 0), (0, 126)))], axis=1)
    slots = {0: packed}
    up = down = packed
    pieces, shard = [], weight
    for step in range(1, 5):
        shares = [(m ^ step, m ^ (step + 4) if step < 4 else m ^ step) for m in range(8)]
        moves = [
            (shares[m][q % 2] + q * 8, m + q * 8) for q in range(4 * RING) for m in range(8)
        ]
        piece = lax.ppermute(shard, ("queue", "mp"), moves)
        up = lax.ppermute(up, "queue", UP)
        if step < 4:
            down = lax.ppermute(down, "queue", DOWN)
            if step == 2:
                near, up = lax.optimization_barrier((near, up))
            piece, up, down, shard = lax.optimization_barrier((piece, up, down, weight))
            slots[step] = down
        slots[-step] = up
        pieces.append(piece)
        if step == 3:
            other_pieces = lax.ppermute(jnp.concatenate(pieces, axis=0), "queue", CORE)
    gathered = [slots[offset] for offset in GATHER]
    far, *_ = lax.optimization_barrier((far, slots[-4], pieces[3], other_pieces))
    far_keys = (far, lax.ppermute(far, "queue", CORE))

    def pick(pair, first, place):
        return pl.pallas_call(
            functools.partial(picked_kernel, rows, first),
            out_shape=jax.ShapeDtypeStruct((total_rows, width), BF16),
            in_specs=[smem()] + [hbm()] * (RING + len(pair)),
            out_specs=vmem(),
            scratch_shapes=[
                pltpu.VMEM((2 * count, width), BF16),
                pltpu.VMEM((total_rows, 128), BF16),
                pltpu.VMEM((total_rows, 128), F32),
                pltpu.VMEM((total_rows, 2 * count), BF16),
                pltpu.SemaphoreType.DMA((RING + len(pair),)),
            ],
            compiler_params=limit(50),
            cost_estimate=pl.CostEstimate(
                flops=first * total_rows * width * count, bytes_accessed=1000, transcendentals=0
            ),
            name="picked",
        )(place, *gathered, *pair)

    gain = norm_gain.reshape(1, width)
    full = jax.ShapeDtypeStruct((total_rows, width), F32)
    narrow = jax.ShapeDtypeStruct((total_rows, 128), F32)
    near_sums, near_table, queries, wanted, own_hidden, full_weight = pl.pallas_call(
        functools.partial(near_kernel, factor, rows),
        out_shape=(
            full,
            narrow,
            jax.ShapeDtypeStruct((total_rows, width), BF16),
            narrow,
            jax.ShapeDtypeStruct((rows, width), F32),
            jax.ShapeDtypeStruct((width, width), BF16),
        ),
        in_specs=[smem()] + [hbm()] * (RING + 8) + [vmem()],
        out_specs=(vmem(),) * 6,
        scratch_shapes=[
            pltpu.VMEM((total_rows, width), BF16),
            pltpu.VMEM((total_rows, width), F32),
            pltpu.VMEM((total_rows, 2 * count), F32),
            pltpu.VMEM((total_rows, 2 * count), BF16),
            pltpu.VMEM((total_rows, 128), BF16),
            pltpu.VMEM((total_rows, 128), F32),
            pltpu.VMEM((2 * count, width), BF16),
            pltpu.SemaphoreType.DMA((2 * RING + 10,)),
        ],
        compiler_params=limit(50),
        cost_estimate=pl.CostEstimate(flops=1000, bytes_accessed=1000, transcendentals=0),
        name="near",
    )(place, *gathered, weight, *pieces, other_pieces, queue_keys, near, gain)

    sums, stats = pl.pallas_call(
        functools.partial(far_kernel, factor),
        out_shape=(full, jax.ShapeDtypeStruct((8, total_rows), F32)),
        in_specs=[smem()] + [hbm()] * 6,
        out_specs=(vmem(),) * 2,
        scratch_shapes=[
            pltpu.VMEM((total_rows, 2 * count), F32),
            pltpu.VMEM((total_rows, 2 * count), BF16),
            pltpu.VMEM((total_rows, 128), F32),
            pltpu.VMEM((total_rows, 128), F32),
            pltpu.VMEM((2 * count, width), BF16),
            pltpu.VMEM((total_rows, width), BF16),
            pltpu.VMEM((total_rows, 128), F32),
            pltpu.VMEM((total_rows, 128), F32),
            pltpu.VMEM((total_rows, width), F32),
            pltpu.SemaphoreType.DMA((6,)),
        ],
        compiler_params=limit(50),
        cost_estimate=pl.CostEstimate(
            flops=8 * total_rows * width * count,
            bytes_accessed=12_000_000,
            transcendentals=total_rows * 2 * count,
        ),
        name="far",
    )(place, *far_keys, queries, wanted, near_table, near_sums)

    def join(*parts):
        return pl.pallas_call(
            functools.partial(join_kernel, len(parts)),
            out_shape=jax.ShapeDtypeStruct(stats.shape, F32),
            in_specs=[vmem()] * len(parts),
            out_specs=vmem(),
            compiler_params=limit(2),
            name="join",
        )(*parts)

    def swap(values, step):
        return lax.ppermute(values, "queue", queue_perm(lambda x, z, c: (x, z ^ step, c)))

    later, stats = lax.optimization_barrier((place, stats))
    other = swap(stats, 1)
    far_picked = pick(far_keys, 2, later)
    other, far_picked = lax.optimization_barrier((other, far_picked))
    pair = join(stats, other)
    later, pair = lax.optimization_barrier((later, pair))
    others = [swap(pair, step) for step in (2, 4, 6)]
    near_picked = pick((queue_keys, near), 0, later)
    near_picked, *others = lax.optimization_barrier((near_picked, *others))
    merged = join(pair, *others)

    *grads, losses = pl.pallas_call(
        functools.partial(scale_kernel, rows),
        out_shape=[jax.ShapeDtypeStruct((rows, width), BF16)] * RING
        + [jax.ShapeDtypeStruct((1, rows), F32)],
        in_specs=[smem()] + [vmem()] * 5,
        out_specs=[vmem()] * (RING + 1),
        scratch_shapes=[pltpu.VMEM((total_rows, 128), F32)],
        compiler_params=limit(16),
        cost_estimate=pl.CostEstimate(
            flops=3 * total_rows * width, bytes_accessed=6_000_000, transcendentals=2000
        ),
        name="scaled",
    )(place, sums, near_picked, far_picked, stats, merged)
    grads = dict(zip(REDUCE, grads))

    def add(first, second):
        return pl.pallas_call(
            add_kernel,
            out_shape=jax.ShapeDtypeStruct((rows, width), BF16),
            in_specs=[vmem()] * 2,
            out_specs=vmem(),
            compiler_params=limit(4),
            cost_estimate=pl.CostEstimate(
                flops=rows * width, bytes_accessed=600_000, transcendentals=0
            ),
            name="add",
        )(first, second)

    shift = (queue_index * count - pointer) % queue_length
    shift = jnp.where(shift >= queue_length - count, shift - queue_length, shift)
    fresh, grads[0] = lax.optimization_barrier((new_keys, grads[0]))
    queue_next = pl.pallas_call(
        queue_kernel,
        out_shape=jax.ShapeDtypeStruct(queue_keys.shape, BF16),
        in_specs=[smem(), vmem(), vmem()],
        out_specs=vmem(),
        compiler_params=limit(12),
        cost_estimate=pl.CostEstimate(
            flops=2 * count * count * width, bytes_accessed=5_000_000, transcendentals=0
        ),
        name="queue",
    )(shift, queue_keys, fresh)

    first, second = grads[4], grads[-3]
    for step in range(4):
        first = lax.ppermute(first, "queue", UP)
        if step == 0:
            first, queue_next = lax.optimization_barrier((first, queue_next))
        if step < 3:
            first = add(first, grads[3 - step])
            second = lax.ppermute(second, "queue", DOWN)
            if step < 2:
                second = add(second, grads[step - 2])

    grad_speech = pl.pallas_call(
        functools.partial(final_kernel, 16.0 * factor),
        out_shape=jax.ShapeDtypeStruct((rows, width), BF16),
        in_specs=[vmem()] * 6,
        out_specs=vmem(),
        compiler_params=limit(8),
        cost_estimate=pl.CostEstimate(
            flops=2 * rows * width * width, bytes_accessed=3_500_000, transcendentals=rows
        ),
        name="final",
    )(first, second, grads[0], own_hidden, gain, full_weight)
    return (losses.reshape(rows), grad_speech, queue_next)


def solution(mesh):
    return jax.shard_map(
        shards,
        mesh=mesh,
        in_specs=(
            P(("queue", "mp"), None),
            P(None, "mp"),
            P(),
            P("queue", None),
            P(),
            P(),
            P(("queue", "mp")),
        ),
        out_specs=(P(("queue", "mp")), P(("queue", "mp"), None), P("queue", None)),
        check_vma=False,
    )
```

```python
import functools
import math

import jax
import jax.numpy as jnp
from jax import lax
from jax.experimental import pallas as pl
from jax.experimental.pallas import tpu as pltpu
from jax.sharding import PartitionSpec as P

RING = 8
BLOCK = 256
F32 = jnp.float32
BF16 = jnp.bfloat16
GATHER = (0, -1, 1, -2, 2, -3, 3, -4)
REDUCE = (4, -3, 3, -2, 2, -1, 1, 0)


def limit(mib):
    return pltpu.CompilerParams(vmem_limit_bytes=mib * 1024 * 1024)


def vmem():
    return pl.BlockSpec(memory_space=pltpu.VMEM)


def hbm():
    return pl.BlockSpec(memory_space=pltpu.HBM)


def smem():
    return pl.BlockSpec(memory_space=pltpu.SMEM)


def queue_perm(move):
    def index(x, z, c):
        return (x * RING + z) * 2 + c

    return [
        (index(x, z, c), index(*move(x, z, c)))
        for x in range(2)
        for z in range(RING)
        for c in range(2)
    ]


UP = queue_perm(lambda x, z, c: (x, (z + 1) % RING, c))
DOWN = queue_perm(lambda x, z, c: (x, (z - 1) % RING, c))
CORE = queue_perm(lambda x, z, c: (x, z, 1 - c))


def start_all(pairs, sems):
    copies = [
        pltpu.make_async_copy(source, target, sems.at[i])
        for i, (source, target) in enumerate(pairs)
    ]
    for copy in copies:
        copy.start()
    return copies


def slot_spans(rows, z):
    return [
        pl.ds(pl.multiple_of(lax.rem(z + offset + RING, RING) * rows, rows), rows)
        for offset in GATHER
    ]


def unpack_ids(codes, wanted):
    values = codes[...].astype(F32)
    wanted[...] = jnp.broadcast_to(values[:, 0:1] * 128.0 + values[:, 1:2], wanted.shape)


def key_pairs(keys, held):
    pairs, start = [], 0
    for source in keys:
        pairs.append((source, held.at[pl.ds(start, source.shape[0]), :]))
        start += source.shape[0]
    return pairs


def picked_kernel(rows, first, place, *refs):
    slots, keys, out = refs[:RING], refs[RING:-6], refs[-6]
    held, codes, wanted, chosen, sems = refs[-5:]
    width, count = out.shape[1], held.shape[0] // 2
    spans = slot_spans(rows, place[0])
    pairs = [
        (slot.at[:, pl.ds(width, 128)], codes.at[span, :]) for slot, span in zip(slots, spans)
    ]
    copies = start_all(pairs + key_pairs(keys, held), sems)
    for copy in copies[:RING]:
        copy.wait()
    copies = copies[RING:]
    unpack_ids(codes, wanted)
    lane = lax.broadcasted_iota(jnp.int32, (BLOCK, 128), 1)
    for b in range(RING * rows // BLOCK):
        span = slice(b * BLOCK, (b + 1) * BLOCK)
        ids = wanted[span, 0:1].astype(jnp.int32)
        total = None
        for j in range(2):
            local = ids - place[3 + first + j]
            for g in range(count // 128):
                mine = lane == local - g * 128
                start = j * count + g * 128
                chosen[span, start : start + 128] = mine.astype(F32).astype(BF16)
            if b == 0:
                share = len(keys) // 2
                for copy in copies[j * share : (j + 1) * share]:
                    copy.wait()
            block = slice(j * count, (j + 1) * count)
            part = jnp.dot(chosen[span, block], held[block, :], preferred_element_type=F32)
            total = part if total is None else total + part
        out[span, :] = total.astype(BF16)


def attend(factor, first, place, queries, wanted, held, scores, probs, peaks, table, keep):
    count = held.shape[0] // 2

    def score(b):
        span = slice(b * BLOCK, (b + 1) * BLOCK)
        top = None
        for j in range(2):
            product = (
                lax.dot_general(
                    queries[span, :],
                    held[j * count : (j + 1) * count, :],
                    (((1,), (1,)), ((), ())),
                    preferred_element_type=F32,
                )
                * factor
            )
            scores[span, j * count : (j + 1) * count] = product
            for g in range(count // 128):
                part = product[:, g * 128 : (g + 1) * 128]
                top = part if top is None else jnp.maximum(top, part)
        peaks[span, :] = top

    def soften(b):
        size = 32
        lane = lax.broadcasted_iota(jnp.int32, (size, 128), 1)
        for q in range(BLOCK // size):
            span = slice(b * BLOCK + q * size, b * BLOCK + (q + 1) * size)
            peak = jnp.max(peaks[span, :], axis=1, keepdims=True)
            ids = wanted[span, 0:1].astype(jnp.int32)
            partial = jnp.zeros((size, 128), F32)
            found = jnp.zeros((size, 128), F32)
            for j in range(2):
                local = ids - place[3 + first + j]
                for g in range(count // 128):
                    columns = slice(j * count + g * 128, j * count + (g + 1) * 128)
                    values = scores[span, columns]
                    powers = jnp.exp(values - peak)
                    probs[span, columns] = powers.astype(BF16)
                    partial += powers
                    found += jnp.where(lane == local - g * 128, values, 0.0)
            total = jnp.sum(partial, axis=1, keepdims=True)
            score_here = jnp.sum(found, axis=1, keepdims=True)
            table[span, :] = jnp.where(
                lane == 0, peak, jnp.where(lane == 1, total, score_here)
            )

    def gather(b):
        span = slice(b * BLOCK, (b + 1) * BLOCK)
        total = None
        for j in range(2):
            block = slice(j * count, (j + 1) * count)
            part = jnp.dot(probs[span, block], held[block, :], preferred_element_type=F32)
            total = part if total is None else total + part
        keep(span, total)

    blocks = queries.shape[0] // BLOCK
    score(0)
    for b in range(blocks):
        if b + 1 < blocks:
            score(b + 1)
        soften(b)
        gather(b)


def near_kernel(factor, rows, place, *refs):
    slots = refs[:RING]
    own_weight, near_weight = refs[RING], refs[RING + 1 : RING + 6]
    keys, gain = refs[RING + 6 : RING + 8], refs[RING + 8]
    sums, table, queries, wanted, own_hidden, full_weight = refs[RING + 9 : RING + 15]
    speech, hidden, scores, probs, codes, peaks, held, sems = refs[RING + 15 :]
    z, mp, core = place[0], place[1], place[2]
    width = hidden.shape[1]
    piece = own_weight.shape[1]
    spans = slot_spans(rows, z)

    def column(step):
        start = pl.multiple_of(jnp.bitwise_xor(mp, step) * piece, piece)
        return full_weight.at[:, pl.ds(start, piece)]

    pairs = []
    for slot, span in zip(slots, spans):
        pairs.append((slot.at[:, pl.ds(0, width)], speech.at[span, :]))
        pairs.append((slot.at[:, pl.ds(width, 128)], codes.at[span, :]))
    pairs += [(own_weight, column(0)), (near_weight[3], column(4))]
    for i in range(3):
        pairs.append((near_weight[i], column(i + 1 + 4 * core)))
        pairs.append((near_weight[4].at[pl.ds(i * width, width), :], column(i + 5 - 4 * core)))
    first = len(pairs)
    copies = start_all(pairs + key_pairs(keys, held), sems)
    for copy in copies[:first]:
        copy.wait()
    unpack_ids(codes, wanted)

    hidden[...] = jnp.dot(speech[...], full_weight[...], preferred_element_type=F32)

    @pl.loop(0, RING)
    def _(b):
        span = pl.ds(pl.multiple_of(b * rows, rows), rows)
        block = hidden[span, :]
        inverse = lax.rsqrt(jnp.mean(block * block, axis=1, keepdims=True) + 1e-06)
        queries[span, :] = (block * inverse * gain[...]).astype(BF16)

    own_hidden[...] = hidden[pl.ds(pl.multiple_of(z * rows, rows), rows), :]
    for copy in copies[first:]:
        copy.wait()

    def keep(span, total):
        sums[span, :] = total

    attend(factor, 0, place, queries, wanted, held, scores, probs, peaks, table, keep)


def far_kernel(factor, place, *refs):
    keys, inputs = refs[:4], refs[4:8]
    sums, stats = refs[8], refs[9]
    scores, probs, peaks, table, held, queries, wanted, before, near_sums, sems = refs[10:]
    holders = (queries, wanted, before, near_sums)
    pairs = list(zip(inputs, holders)) + key_pairs(keys, held)
    for copy in start_all(pairs, sems):
        copy.wait()

    def keep(span, total):
        near, far = before[span, :], table[span, :]
        peak = jnp.maximum(near[:, 0:1], far[:, 0:1])
        left, right = jnp.exp(near[:, 0:1] - peak), jnp.exp(far[:, 0:1] - peak)
        sums[span, :] = near_sums[span, :] * left + total * right
        lane = lax.broadcasted_iota(jnp.int32, near.shape, 1)
        table[span, :] = jnp.where(
            lane == 0, peak, jnp.where(lane == 1, near * left + far * right, near + far)
        )

    attend(factor, 2, place, queries, wanted, held, scores, probs, peaks, table, keep)
    stats[...] = table[...].T[:8, :]


def join_kernel(count, *refs):
    parts, out = refs[:count], refs[count]
    peak = parts[0][0:1, :]
    for part in parts[1:]:
        peak = jnp.maximum(peak, part[0:1, :])
    total = found = 0.0
    for part in parts:
        total += part[1:2, :] * jnp.exp(part[0:1, :] - peak)
        found += part[2:3, :]
    row = lax.broadcasted_iota(jnp.int32, out.shape, 0)
    out[...] = jnp.where(row == 0, peak, jnp.where(row == 1, total, found))


def scale_kernel(rows, place, sums, near_picked, far_picked, local, merged, *refs):
    outs, loss, table = refs[:RING], refs[RING], refs[RING + 1]
    log_total = merged[0:1, :] + jnp.log(merged[1:2, :])
    scale = jnp.exp(local[0:1, :] - log_total)
    losses = log_total - merged[2:3, :]
    row = lax.broadcasted_iota(jnp.int32, (128, scale.shape[1]), 0)
    table[...] = jnp.where(row == 0, scale, losses).T

    def span_of(offset):
        start = lax.rem(place[0] + offset + RING, RING) * rows
        return pl.ds(pl.multiple_of(start, rows), rows)

    for slot, offset in enumerate(REDUCE):
        span = span_of(offset)
        picked = near_picked[span, :].astype(F32) + far_picked[span, :].astype(F32)
        outs[slot][...] = (table[span, 0:1] * sums[span, :] - picked).astype(BF16)
    own = jnp.broadcast_to(table[span_of(0), 1:2], (rows, 128))
    loss[...] = own.T[:1, :]


def add_kernel(first, second, out):
    out[...] = (first[...].astype(F32) + second[...].astype(F32)).astype(BF16)


def final_kernel(factor, first, second, own, hidden, gain, weight, out):
    width = hidden.shape[1]
    grad = (first[...].astype(F32) + second[...].astype(F32) + own[...].astype(F32)) * factor
    scaled = gain[...] * grad
    values = hidden[...]
    inverse = lax.rsqrt(jnp.mean(values * values, axis=1, keepdims=True) + 1e-06)
    inner = jnp.sum(scaled * values, axis=1, keepdims=True)
    hidden_grad = (
        inverse * scaled - values * (inverse * inverse * inverse) * inner / width
    ).astype(BF16)
    out[...] = lax.dot_general(
        hidden_grad, weight[...], (((1,), (1,)), ((), ())), preferred_element_type=F32
    ).astype(BF16)


def queue_kernel(shift, keys, fresh, out):
    count = keys.shape[0]
    wanted = lax.broadcasted_iota(jnp.int32, (count, 1), 0) + shift[0]
    pick = lax.broadcasted_iota(jnp.int32, (count, fresh.shape[0]), 1) == wanted
    moved = jnp.dot(pick.astype(F32).astype(BF16), fresh[...], preferred_element_type=F32)
    replaced = (wanted >= 0) & (wanted < fresh.shape[0])
    out[...] = jnp.where(replaced, moved, keys[...].astype(F32)).astype(BF16)


def shards(speech, weight, norm_gain, queue_keys, new_keys, pointer, positives):
    rows, width = speech.shape
    count = queue_keys.shape[0]
    total_rows = RING * rows
    queue_length = count * lax.axis_size("queue")
    queue_index = lax.axis_index("queue")
    mp = lax.axis_index("mp")
    z = (queue_index // 2) % RING
    factor = 2.0 / math.sqrt(width)

    core = queue_index % 2
    half = RING * 2
    across = [
        (q * 8 + m, (q ^ half) * 8 + (m ^ 4)) for q in range(4 * RING) for m in range(8)
    ]
    part = count // 2
    far_first = lax.ppermute(queue_keys[:part], ("queue", "mp"), across)
    far_last = lax.ppermute(queue_keys[part:], ("queue", "mp"), across)
    near = lax.ppermute(queue_keys, "queue", CORE)
    flipped = queue_index ^ (2 * RING)
    bases = [index * count for index in (queue_index, queue_index ^ 1, flipped, flipped ^ 1)]
    place = jnp.stack([z, mp, core] + bases).astype(jnp.int32)

    codes = jnp.stack([positives // 128, positives % 128], axis=1).astype(BF16)
    packed = jnp.concatenate([speech, jnp.pad(codes, ((0, 0), (0, 126)))], axis=1)
    slots = {0: packed}
    up = down = packed
    pieces, shard = [], weight
    for step in range(1, 5):
        shares = [(m ^ step, m ^ (step + 4) if step < 4 else m ^ step) for m in range(8)]
        moves = [
            (shares[m][q % 2] + q * 8, m + q * 8) for q in range(4 * RING) for m in range(8)
        ]
        piece = lax.ppermute(shard, ("queue", "mp"), moves)
        up = lax.ppermute(up, "queue", UP)
        if step < 4:
            down = lax.ppermute(down, "queue", DOWN)
            if step == 2:
                near, up = lax.optimization_barrier((near, up))
            piece, up, down, shard = lax.optimization_barrier((piece, up, down, weight))
            if step == 2:
                far_first, up, shard = lax.optimization_barrier((far_first, up, shard))
            slots[step] = down
        slots[-step] = up
        pieces.append(piece)
        if step == 3:
            other_pieces = lax.ppermute(jnp.concatenate(pieces, axis=0), "queue", CORE)
    gathered = [slots[offset] for offset in GATHER]
    far_last, *_ = lax.optimization_barrier((far_last, slots[-4], pieces[3], other_pieces))
    far_keys = (
        far_first,
        far_last,
        lax.ppermute(far_first, "queue", CORE),
        lax.ppermute(far_last, "queue", CORE),
    )

    def pick(pair, first, place):
        return pl.pallas_call(
            functools.partial(picked_kernel, rows, first),
            out_shape=jax.ShapeDtypeStruct((total_rows, width), BF16),
            in_specs=[smem()] + [hbm()] * (RING + len(pair)),
            out_specs=vmem(),
            scratch_shapes=[
                pltpu.VMEM((2 * count, width), BF16),
                pltpu.VMEM((total_rows, 128), BF16),
                pltpu.VMEM((total_rows, 128), F32),
                pltpu.VMEM((total_rows, 2 * count), BF16),
                pltpu.SemaphoreType.DMA((RING + len(pair),)),
            ],
            compiler_params=limit(50),
            cost_estimate=pl.CostEstimate(
                flops=first * total_rows * width * count, bytes_accessed=1000, transcendentals=0
            ),
            name="picked",
        )(place, *gathered, *pair)

    gain = norm_gain.reshape(1, width)
    full = jax.ShapeDtypeStruct((total_rows, width), F32)
    narrow = jax.ShapeDtypeStruct((total_rows, 128), F32)
    near_sums, near_table, queries, wanted, own_hidden, full_weight = pl.pallas_call(
        functools.partial(near_kernel, factor, rows),
        out_shape=(
            full,
            narrow,
            jax.ShapeDtypeStruct((total_rows, width), BF16),
            narrow,
            jax.ShapeDtypeStruct((rows, width), F32),
            jax.ShapeDtypeStruct((width, width), BF16),
        ),
        in_specs=[smem()] + [hbm()] * (RING + 8) + [vmem()],
        out_specs=(vmem(),) * 6,
        scratch_shapes=[
            pltpu.VMEM((total_rows, width), BF16),
            pltpu.VMEM((total_rows, width), F32),
            pltpu.VMEM((total_rows, 2 * count), F32),
            pltpu.VMEM((total_rows, 2 * count), BF16),
            pltpu.VMEM((total_rows, 128), BF16),
            pltpu.VMEM((total_rows, 128), F32),
            pltpu.VMEM((2 * count, width), BF16),
            pltpu.SemaphoreType.DMA((2 * RING + 10,)),
        ],
        compiler_params=limit(50),
        cost_estimate=pl.CostEstimate(flops=1000, bytes_accessed=1000, transcendentals=0),
        name="near",
    )(place, *gathered, weight, *pieces, other_pieces, queue_keys, near, gain)

    sums, stats = pl.pallas_call(
        functools.partial(far_kernel, factor),
        out_shape=(full, jax.ShapeDtypeStruct((8, total_rows), F32)),
        in_specs=[smem()] + [hbm()] * 8,
        out_specs=(vmem(),) * 2,
        scratch_shapes=[
            pltpu.VMEM((total_rows, 2 * count), F32),
            pltpu.VMEM((total_rows, 2 * count), BF16),
            pltpu.VMEM((total_rows, 128), F32),
            pltpu.VMEM((total_rows, 128), F32),
            pltpu.VMEM((2 * count, width), BF16),
            pltpu.VMEM((total_rows, width), BF16),
            pltpu.VMEM((total_rows, 128), F32),
            pltpu.VMEM((total_rows, 128), F32),
            pltpu.VMEM((total_rows, width), F32),
            pltpu.SemaphoreType.DMA((8,)),
        ],
        compiler_params=limit(50),
        cost_estimate=pl.CostEstimate(
            flops=8 * total_rows * width * count,
            bytes_accessed=12_000_000,
            transcendentals=total_rows * 2 * count,
        ),
        name="far",
    )(place, *far_keys, queries, wanted, near_table, near_sums)

    def join(*parts):
        return pl.pallas_call(
            functools.partial(join_kernel, len(parts)),
            out_shape=jax.ShapeDtypeStruct(stats.shape, F32),
            in_specs=[vmem()] * len(parts),
            out_specs=vmem(),
            compiler_params=limit(2),
            name="join",
        )(*parts)

    def swap(values, step):
        return lax.ppermute(values, "queue", queue_perm(lambda x, z, c: (x, z ^ step, c)))

    later, stats = lax.optimization_barrier((place, stats))
    other = swap(stats, 1)
    far_picked = pick(far_keys, 2, later)
    other, far_picked = lax.optimization_barrier((other, far_picked))
    pair = join(stats, other)
    later, pair = lax.optimization_barrier((later, pair))
    others = [swap(pair, step) for step in (2, 4, 6)]
    near_picked = pick((queue_keys, near), 0, later)
    near_picked, *others = lax.optimization_barrier((near_picked, *others))
    merged = join(pair, *others)

    *grads, losses = pl.pallas_call(
        functools.partial(scale_kernel, rows),
        out_shape=[jax.ShapeDtypeStruct((rows, width), BF16)] * RING
        + [jax.ShapeDtypeStruct((1, rows), F32)],
        in_specs=[smem()] + [vmem()] * 5,
        out_specs=[vmem()] * (RING + 1),
        scratch_shapes=[pltpu.VMEM((total_rows, 128), F32)],
        compiler_params=limit(16),
        cost_estimate=pl.CostEstimate(
            flops=3 * total_rows * width, bytes_accessed=6_000_000, transcendentals=2000
        ),
        name="scaled",
    )(place, sums, near_picked, far_picked, stats, merged)
    grads = dict(zip(REDUCE, grads))

    def add(first, second):
        return pl.pallas_call(
            add_kernel,
            out_shape=jax.ShapeDtypeStruct((rows, width), BF16),
            in_specs=[vmem()] * 2,
            out_specs=vmem(),
            compiler_params=limit(4),
            cost_estimate=pl.CostEstimate(
                flops=rows * width, bytes_accessed=600_000, transcendentals=0
            ),
            name="add",
        )(first, second)

    shift = (queue_index * count - pointer) % queue_length
    shift = jnp.where(shift >= queue_length - count, shift - queue_length, shift)
    fresh, grads[0] = lax.optimization_barrier((new_keys, grads[0]))
    queue_next = pl.pallas_call(
        queue_kernel,
        out_shape=jax.ShapeDtypeStruct(queue_keys.shape, BF16),
        in_specs=[smem(), vmem(), vmem()],
        out_specs=vmem(),
        compiler_params=limit(12),
        cost_estimate=pl.CostEstimate(
            flops=2 * count * count * width, bytes_accessed=5_000_000, transcendentals=0
        ),
        name="queue",
    )(shift, queue_keys, fresh)

    first, second = grads[4], grads[-3]
    for step in range(4):
        first = lax.ppermute(first, "queue", UP)
        if step == 0:
            first, queue_next = lax.optimization_barrier((first, queue_next))
        if step < 3:
            first = add(first, grads[3 - step])
            second = lax.ppermute(second, "queue", DOWN)
            if step < 2:
                second = add(second, grads[step - 2])

    grad_speech = pl.pallas_call(
        functools.partial(final_kernel, 16.0 * factor),
        out_shape=jax.ShapeDtypeStruct((rows, width), BF16),
        in_specs=[vmem()] * 6,
        out_specs=vmem(),
        compiler_params=limit(8),
        cost_estimate=pl.CostEstimate(
            flops=2 * rows * width * width, bytes_accessed=3_500_000, transcendentals=rows
        ),
        name="final",
    )(first, second, grads[0], own_hidden, gain, full_weight)
    return (losses.reshape(rows), grad_speech, queue_next)


def solution(mesh):
    return jax.shard_map(
        shards,
        mesh=mesh,
        in_specs=(
            P(("queue", "mp"), None),
            P(None, "mp"),
            P(),
            P("queue", None),
            P(),
            P(),
            P(("queue", "mp")),
        ),
        out_specs=(P(("queue", "mp")), P(("queue", "mp"), None), P("queue", None)),
        check_vma=False,
    )
```

```python
import functools
import math

import jax
import jax.numpy as jnp
from jax import lax
from jax.experimental import pallas as pl
from jax.experimental.pallas import tpu as pltpu
from jax.sharding import PartitionSpec as P

RING = 8
BLOCK = 256
F32 = jnp.float32
BF16 = jnp.bfloat16
GATHER = (0, -1, 1, -2, 2, -3, 3, -4)
REDUCE = (4, -3, 3, -2, 2, -1, 1, 0)


def limit(mib):
    return pltpu.CompilerParams(vmem_limit_bytes=mib * 1024 * 1024)


def vmem():
    return pl.BlockSpec(memory_space=pltpu.VMEM)


def hbm():
    return pl.BlockSpec(memory_space=pltpu.HBM)


def smem():
    return pl.BlockSpec(memory_space=pltpu.SMEM)


def queue_perm(move):
    def index(x, z, c):
        return (x * RING + z) * 2 + c

    return [
        (index(x, z, c), index(*move(x, z, c)))
        for x in range(2)
        for z in range(RING)
        for c in range(2)
    ]


UP = queue_perm(lambda x, z, c: (x, (z + 1) % RING, c))
DOWN = queue_perm(lambda x, z, c: (x, (z - 1) % RING, c))
CORE = queue_perm(lambda x, z, c: (x, z, 1 - c))


def start_all(pairs, sems):
    copies = [
        pltpu.make_async_copy(source, target, sems.at[i])
        for i, (source, target) in enumerate(pairs)
    ]
    for copy in copies:
        copy.start()
    return copies


def slot_spans(rows, z):
    return [
        pl.ds(pl.multiple_of(lax.rem(z + offset + RING, RING) * rows, rows), rows)
        for offset in GATHER
    ]


def unpack_ids(codes, wanted):
    values = codes[...].astype(F32)
    wanted[...] = jnp.broadcast_to(values[:, 0:1] * 128.0 + values[:, 1:2], wanted.shape)


def key_pairs(keys, held):
    pairs, start = [], 0
    for source in keys:
        pairs.append((source, held.at[pl.ds(start, source.shape[0]), :]))
        start += source.shape[0]
    return pairs


def picked_kernel(rows, first, place, *refs):
    slots, keys, out = refs[:RING], refs[RING:-6], refs[-6]
    held, codes, wanted, chosen, sems = refs[-5:]
    width, count = out.shape[1], held.shape[0] // 2
    spans = slot_spans(rows, place[0])
    pairs = [
        (slot.at[:, pl.ds(width, 128)], codes.at[span, :]) for slot, span in zip(slots, spans)
    ]
    copies = start_all(pairs + key_pairs(keys, held), sems)
    for copy in copies[:RING]:
        copy.wait()
    copies = copies[RING:]
    unpack_ids(codes, wanted)
    lane = lax.broadcasted_iota(jnp.int32, (BLOCK, 128), 1)
    for b in range(RING * rows // BLOCK):
        span = slice(b * BLOCK, (b + 1) * BLOCK)
        ids = wanted[span, 0:1].astype(jnp.int32)
        total = None
        for j in range(2):
            local = ids - place[3 + first + j]
            for g in range(count // 128):
                mine = lane == local - g * 128
                start = j * count + g * 128
                chosen[span, start : start + 128] = mine.astype(F32).astype(BF16)
            if b == 0:
                share = len(keys) // 2
                for copy in copies[j * share : (j + 1) * share]:
                    copy.wait()
            block = slice(j * count, (j + 1) * count)
            part = jnp.dot(chosen[span, block], held[block, :], preferred_element_type=F32)
            total = part if total is None else total + part
        out[span, :] = total.astype(BF16)


def attend(factor, first, place, queries, wanted, held, scores, probs, peaks, table, keep):
    count = held.shape[0] // 2

    def score(b):
        span = slice(b * BLOCK, (b + 1) * BLOCK)
        top = None
        for j in range(2):
            product = (
                lax.dot_general(
                    queries[span, :],
                    held[j * count : (j + 1) * count, :],
                    (((1,), (1,)), ((), ())),
                    preferred_element_type=F32,
                )
                * factor
            )
            scores[span, j * count : (j + 1) * count] = product
            for g in range(count // 128):
                part = product[:, g * 128 : (g + 1) * 128]
                top = part if top is None else jnp.maximum(top, part)
        peaks[span, :] = top

    def soften(b):
        size = 32
        lane = lax.broadcasted_iota(jnp.int32, (size, 128), 1)
        for q in range(BLOCK // size):
            span = slice(b * BLOCK + q * size, b * BLOCK + (q + 1) * size)
            peak = jnp.max(peaks[span, :], axis=1, keepdims=True)
            ids = wanted[span, 0:1].astype(jnp.int32)
            partial = jnp.zeros((size, 128), F32)
            found = jnp.zeros((size, 128), F32)
            for j in range(2):
                local = ids - place[3 + first + j]
                for g in range(count // 128):
                    columns = slice(j * count + g * 128, j * count + (g + 1) * 128)
                    values = scores[span, columns]
                    powers = jnp.exp(values - peak)
                    probs[span, columns] = powers.astype(BF16)
                    partial += powers
                    found += jnp.where(lane == local - g * 128, values, 0.0)
            total = jnp.sum(partial, axis=1, keepdims=True)
            score_here = jnp.sum(found, axis=1, keepdims=True)
            table[span, :] = jnp.where(
                lane == 0, peak, jnp.where(lane == 1, total, score_here)
            )

    def gather(b):
        span = slice(b * BLOCK, (b + 1) * BLOCK)
        total = None
        for j in range(2):
            block = slice(j * count, (j + 1) * count)
            part = jnp.dot(probs[span, block], held[block, :], preferred_element_type=F32)
            total = part if total is None else total + part
        keep(span, total)

    blocks = queries.shape[0] // BLOCK
    score(0)
    for b in range(blocks):
        if b + 1 < blocks:
            score(b + 1)
        soften(b)
        gather(b)


def near_kernel(factor, rows, place, *refs):
    slots = refs[:RING]
    own_weight, near_weight = refs[RING], refs[RING + 1 : RING + 6]
    keys, gain = refs[RING + 6 : RING + 8], refs[RING + 8]
    sums, table, queries, wanted, own_hidden, full_weight = refs[RING + 9 : RING + 15]
    speech, hidden, scores, probs, codes, peaks, held, sems = refs[RING + 15 :]
    z, mp, core = place[0], place[1], place[2]
    width = hidden.shape[1]
    piece = own_weight.shape[1]
    spans = slot_spans(rows, z)

    def column(step):
        start = pl.multiple_of(jnp.bitwise_xor(mp, step) * piece, piece)
        return full_weight.at[:, pl.ds(start, piece)]

    pairs = []
    for slot, span in zip(slots, spans):
        pairs.append((slot.at[:, pl.ds(0, width)], speech.at[span, :]))
        pairs.append((slot.at[:, pl.ds(width, 128)], codes.at[span, :]))
    pairs += [(own_weight, column(0)), (near_weight[3], column(4))]
    for i in range(3):
        pairs.append((near_weight[i], column(i + 1 + 4 * core)))
        pairs.append((near_weight[4].at[pl.ds(i * width, width), :], column(i + 5 - 4 * core)))
    first = len(pairs)
    copies = start_all(pairs + key_pairs(keys, held), sems)
    for copy in copies[:first]:
        copy.wait()
    unpack_ids(codes, wanted)

    hidden[...] = jnp.dot(speech[...], full_weight[...], preferred_element_type=F32)

    @pl.loop(0, RING)
    def _(b):
        span = pl.ds(pl.multiple_of(b * rows, rows), rows)
        block = hidden[span, :]
        inverse = lax.rsqrt(jnp.mean(block * block, axis=1, keepdims=True) + 1e-06)
        queries[span, :] = (block * inverse * gain[...]).astype(BF16)

    own_hidden[...] = hidden[pl.ds(pl.multiple_of(z * rows, rows), rows), :]
    for copy in copies[first:]:
        copy.wait()

    def keep(span, total):
        sums[span, :] = total

    attend(factor, 0, place, queries, wanted, held, scores, probs, peaks, table, keep)


def far_kernel(factor, place, *refs):
    keys, inputs = refs[:4], refs[4:8]
    sums, stats = refs[8], refs[9]
    scores, probs, peaks, table, held, queries, wanted, before, near_sums, sems = refs[10:]
    holders = (queries, wanted, before, near_sums)
    pairs = list(zip(inputs, holders)) + key_pairs(keys, held)
    for copy in start_all(pairs, sems):
        copy.wait()

    def keep(span, total):
        near, far = before[span, :], table[span, :]
        peak = jnp.maximum(near[:, 0:1], far[:, 0:1])
        left, right = jnp.exp(near[:, 0:1] - peak), jnp.exp(far[:, 0:1] - peak)
        sums[span, :] = near_sums[span, :] * left + total * right
        lane = lax.broadcasted_iota(jnp.int32, near.shape, 1)
        table[span, :] = jnp.where(
            lane == 0, peak, jnp.where(lane == 1, near * left + far * right, near + far)
        )

    attend(factor, 2, place, queries, wanted, held, scores, probs, peaks, table, keep)
    stats[...] = table[...].T[:8, :]


def join_kernel(count, *refs):
    parts, out = refs[:count], refs[count]
    peak = parts[0][0:1, :]
    for part in parts[1:]:
        peak = jnp.maximum(peak, part[0:1, :])
    total = found = 0.0
    for part in parts:
        total += part[1:2, :] * jnp.exp(part[0:1, :] - peak)
        found += part[2:3, :]
    row = lax.broadcasted_iota(jnp.int32, out.shape, 0)
    out[...] = jnp.where(row == 0, peak, jnp.where(row == 1, total, found))


def scale_kernel(rows, place, sums, near_picked, far_picked, local, merged, *refs):
    outs, loss, table = refs[:RING], refs[RING], refs[RING + 1]
    log_total = merged[0:1, :] + jnp.log(merged[1:2, :])
    scale = jnp.exp(local[0:1, :] - log_total)
    losses = log_total - merged[2:3, :]
    row = lax.broadcasted_iota(jnp.int32, (128, scale.shape[1]), 0)
    table[...] = jnp.where(row == 0, scale, losses).T

    def span_of(offset):
        start = lax.rem(place[0] + offset + RING, RING) * rows
        return pl.ds(pl.multiple_of(start, rows), rows)

    for slot, offset in enumerate(REDUCE):
        span = span_of(offset)
        picked = near_picked[span, :].astype(F32) + far_picked[span, :].astype(F32)
        outs[slot][...] = (table[span, 0:1] * sums[span, :] - picked).astype(BF16)
    own = jnp.broadcast_to(table[span_of(0), 1:2], (rows, 128))
    loss[...] = own.T[:1, :]


def add_kernel(first, second, out):
    out[...] = (first[...].astype(F32) + second[...].astype(F32)).astype(BF16)


def final_kernel(factor, first, second, own, hidden, gain, weight, out):
    width = hidden.shape[1]
    grad = (first[...].astype(F32) + second[...].astype(F32) + own[...].astype(F32)) * factor
    scaled = gain[...] * grad
    values = hidden[...]
    inverse = lax.rsqrt(jnp.mean(values * values, axis=1, keepdims=True) + 1e-06)
    inner = jnp.sum(scaled * values, axis=1, keepdims=True)
    hidden_grad = (
        inverse * scaled - values * (inverse * inverse * inverse) * inner / width
    ).astype(BF16)
    out[...] = lax.dot_general(
        hidden_grad, weight[...], (((1,), (1,)), ((), ())), preferred_element_type=F32
    ).astype(BF16)


def queue_kernel(shift, keys, fresh, out):
    count = keys.shape[0]
    wanted = lax.broadcasted_iota(jnp.int32, (count, 1), 0) + shift[0]
    pick = lax.broadcasted_iota(jnp.int32, (count, fresh.shape[0]), 1) == wanted
    moved = jnp.dot(pick.astype(F32).astype(BF16), fresh[...], preferred_element_type=F32)
    replaced = (wanted >= 0) & (wanted < fresh.shape[0])
    out[...] = jnp.where(replaced, moved, keys[...].astype(F32)).astype(BF16)


def shards(speech, weight, norm_gain, queue_keys, new_keys, pointer, positives):
    rows, width = speech.shape
    count = queue_keys.shape[0]
    total_rows = RING * rows
    queue_length = count * lax.axis_size("queue")
    queue_index = lax.axis_index("queue")
    mp = lax.axis_index("mp")
    z = (queue_index // 2) % RING
    factor = 2.0 / math.sqrt(width)

    core = queue_index % 2
    half = RING * 2
    across = [
        (q * 8 + m, (q ^ half) * 8 + (m ^ 4)) for q in range(4 * RING) for m in range(8)
    ]
    part = count * 2 // 3
    far_first = lax.ppermute(queue_keys[:part], ("queue", "mp"), across)
    far_last = lax.ppermute(queue_keys[part:], ("queue", "mp"), across)
    near = lax.ppermute(queue_keys, "queue", CORE)
    flipped = queue_index ^ (2 * RING)
    bases = [index * count for index in (queue_index, queue_index ^ 1, flipped, flipped ^ 1)]
    place = jnp.stack([z, mp, core] + bases).astype(jnp.int32)

    codes = jnp.stack([positives // 128, positives % 128], axis=1).astype(BF16)
    packed = jnp.concatenate([speech, jnp.pad(codes, ((0, 0), (0, 126)))], axis=1)
    slots = {0: packed}
    up = down = packed
    pieces, shard = [], weight
    for step in range(1, 5):
        shares = [(m ^ step, m ^ (step + 4) if step < 4 else m ^ step) for m in range(8)]
        moves = [
            (shares[m][q % 2] + q * 8, m + q * 8) for q in range(4 * RING) for m in range(8)
        ]
        piece = lax.ppermute(shard, ("queue", "mp"), moves)
        up = lax.ppermute(up, "queue", UP)
        if step < 4:
            down = lax.ppermute(down, "queue", DOWN)
            if step == 2:
                near, up = lax.optimization_barrier((near, up))
            piece, up, down, shard = lax.optimization_barrier((piece, up, down, weight))
            if step == 2:
                far_first, up, shard = lax.optimization_barrier((far_first, up, shard))
            slots[step] = down
        slots[-step] = up
        pieces.append(piece)
        if step == 3:
            other_pieces = lax.ppermute(jnp.concatenate(pieces, axis=0), "queue", CORE)
    gathered = [slots[offset] for offset in GATHER]
    far_first, *_ = lax.optimization_barrier((far_first, slots[-4], pieces[3], other_pieces))
    far_near_first = lax.ppermute(far_first, "queue", CORE)

    def pick(pair, first, place):
        return pl.pallas_call(
            functools.partial(picked_kernel, rows, first),
            out_shape=jax.ShapeDtypeStruct((total_rows, width), BF16),
            in_specs=[smem()] + [hbm()] * (RING + len(pair)),
            out_specs=vmem(),
            scratch_shapes=[
                pltpu.VMEM((2 * count, width), BF16),
                pltpu.VMEM((total_rows, 128), BF16),
                pltpu.VMEM((total_rows, 128), F32),
                pltpu.VMEM((total_rows, 2 * count), BF16),
                pltpu.SemaphoreType.DMA((RING + len(pair),)),
            ],
            compiler_params=limit(50),
            cost_estimate=pl.CostEstimate(
                flops=first * total_rows * width * count, bytes_accessed=1000, transcendentals=0
            ),
            name="picked",
        )(place, *gathered, *pair)

    gain = norm_gain.reshape(1, width)
    full = jax.ShapeDtypeStruct((total_rows, width), F32)
    narrow = jax.ShapeDtypeStruct((total_rows, 128), F32)
    near_sums, near_table, queries, wanted, own_hidden, full_weight = pl.pallas_call(
        functools.partial(near_kernel, factor, rows),
        out_shape=(
            full,
            narrow,
            jax.ShapeDtypeStruct((total_rows, width), BF16),
            narrow,
            jax.ShapeDtypeStruct((rows, width), F32),
            jax.ShapeDtypeStruct((width, width), BF16),
        ),
        in_specs=[smem()] + [hbm()] * (RING + 8) + [vmem()],
        out_specs=(vmem(),) * 6,
        scratch_shapes=[
            pltpu.VMEM((total_rows, width), BF16),
            pltpu.VMEM((total_rows, width), F32),
            pltpu.VMEM((total_rows, 2 * count), F32),
            pltpu.VMEM((total_rows, 2 * count), BF16),
            pltpu.VMEM((total_rows, 128), BF16),
            pltpu.VMEM((total_rows, 128), F32),
            pltpu.VMEM((2 * count, width), BF16),
            pltpu.SemaphoreType.DMA((2 * RING + 10,)),
        ],
        compiler_params=limit(50),
        cost_estimate=pl.CostEstimate(flops=1000, bytes_accessed=1000, transcendentals=0),
        name="near",
    )(place, *gathered, weight, *pieces, other_pieces, queue_keys, near, gain)

    far_last, near_table = lax.optimization_barrier((far_last, near_table))
    far_keys = (far_first, far_last, far_near_first, lax.ppermute(far_last, "queue", CORE))
    sums, stats = pl.pallas_call(
        functools.partial(far_kernel, factor),
        out_shape=(full, jax.ShapeDtypeStruct((8, total_rows), F32)),
        in_specs=[smem()] + [hbm()] * 8,
        out_specs=(vmem(),) * 2,
        scratch_shapes=[
            pltpu.VMEM((total_rows, 2 * count), F32),
            pltpu.VMEM((total_rows, 2 * count), BF16),
            pltpu.VMEM((total_rows, 128), F32),
            pltpu.VMEM((total_rows, 128), F32),
            pltpu.VMEM((2 * count, width), BF16),
            pltpu.VMEM((total_rows, width), BF16),
            pltpu.VMEM((total_rows, 128), F32),
            pltpu.VMEM((total_rows, 128), F32),
            pltpu.VMEM((total_rows, width), F32),
            pltpu.SemaphoreType.DMA((8,)),
        ],
        compiler_params=limit(50),
        cost_estimate=pl.CostEstimate(
            flops=8 * total_rows * width * count,
            bytes_accessed=12_000_000,
            transcendentals=total_rows * 2 * count,
        ),
        name="far",
    )(place, *far_keys, queries, wanted, near_table, near_sums)

    def join(*parts):
        return pl.pallas_call(
            functools.partial(join_kernel, len(parts)),
            out_shape=jax.ShapeDtypeStruct(stats.shape, F32),
            in_specs=[vmem()] * len(parts),
            out_specs=vmem(),
            compiler_params=limit(2),
            name="join",
        )(*parts)

    def swap(values, step):
        return lax.ppermute(values, "queue", queue_perm(lambda x, z, c: (x, z ^ step, c)))

    later, stats = lax.optimization_barrier((place, stats))
    other = swap(stats, 1)
    far_picked = pick(far_keys, 2, later)
    other, far_picked = lax.optimization_barrier((other, far_picked))
    pair = join(stats, other)
    later, pair = lax.optimization_barrier((later, pair))
    others = [swap(pair, step) for step in (2, 4, 6)]
    near_picked = pick((queue_keys, near), 0, later)
    near_picked, *others = lax.optimization_barrier((near_picked, *others))
    merged = join(pair, *others)

    *grads, losses = pl.pallas_call(
        functools.partial(scale_kernel, rows),
        out_shape=[jax.ShapeDtypeStruct((rows, width), BF16)] * RING
        + [jax.ShapeDtypeStruct((1, rows), F32)],
        in_specs=[smem()] + [vmem()] * 5,
        out_specs=[vmem()] * (RING + 1),
        scratch_shapes=[pltpu.VMEM((total_rows, 128), F32)],
        compiler_params=limit(16),
        cost_estimate=pl.CostEstimate(
            flops=3 * total_rows * width, bytes_accessed=6_000_000, transcendentals=2000
        ),
        name="scaled",
    )(place, sums, near_picked, far_picked, stats, merged)
    grads = dict(zip(REDUCE, grads))

    def add(first, second):
        return pl.pallas_call(
            add_kernel,
            out_shape=jax.ShapeDtypeStruct((rows, width), BF16),
            in_specs=[vmem()] * 2,
            out_specs=vmem(),
            compiler_params=limit(4),
            cost_estimate=pl.CostEstimate(
                flops=rows * width, bytes_accessed=600_000, transcendentals=0
            ),
            name="add",
        )(first, second)

    shift = (queue_index * count - pointer) % queue_length
    shift = jnp.where(shift >= queue_length - count, shift - queue_length, shift)
    fresh, grads[0] = lax.optimization_barrier((new_keys, grads[0]))
    queue_next = pl.pallas_call(
        queue_kernel,
        out_shape=jax.ShapeDtypeStruct(queue_keys.shape, BF16),
        in_specs=[smem(), vmem(), vmem()],
        out_specs=vmem(),
        compiler_params=limit(12),
        cost_estimate=pl.CostEstimate(
            flops=2 * count * count * width, bytes_accessed=5_000_000, transcendentals=0
        ),
        name="queue",
    )(shift, queue_keys, fresh)

    first, second = grads[4], grads[-3]
    for step in range(4):
        first = lax.ppermute(first, "queue", UP)
        if step == 0:
            first, queue_next = lax.optimization_barrier((first, queue_next))
        if step < 3:
            first = add(first, grads[3 - step])
            second = lax.ppermute(second, "queue", DOWN)
            if step < 2:
                second = add(second, grads[step - 2])

    grad_speech = pl.pallas_call(
        functools.partial(final_kernel, 16.0 * factor),
        out_shape=jax.ShapeDtypeStruct((rows, width), BF16),
        in_specs=[vmem()] * 6,
        out_specs=vmem(),
        compiler_params=limit(8),
        cost_estimate=pl.CostEstimate(
            flops=2 * rows * width * width, bytes_accessed=3_500_000, transcendentals=rows
        ),
        name="final",
    )(first, second, grads[0], own_hidden, gain, full_weight)
    return (losses.reshape(rows), grad_speech, queue_next)


def solution(mesh):
    return jax.shard_map(
        shards,
        mesh=mesh,
        in_specs=(
            P(("queue", "mp"), None),
            P(None, "mp"),
            P(),
            P("queue", None),
            P(),
            P(),
            P(("queue", "mp")),
        ),
        out_specs=(P(("queue", "mp")), P(("queue", "mp"), None), P("queue", None)),
        check_vma=False,
    )
```

```python
import functools
import math

import jax
import jax.numpy as jnp
from jax import lax
from jax.experimental import pallas as pl
from jax.experimental.pallas import tpu as pltpu
from jax.sharding import PartitionSpec as P

RING = 8
BLOCK = 256
F32 = jnp.float32
BF16 = jnp.bfloat16
GATHER = (0, -1, 1, -2, 2, -3, 3, -4)
REDUCE = (4, -3, 3, -2, 2, -1, 1, 0)


def limit(mib):
    return pltpu.CompilerParams(vmem_limit_bytes=mib * 1024 * 1024)


def vmem():
    return pl.BlockSpec(memory_space=pltpu.VMEM)


def hbm():
    return pl.BlockSpec(memory_space=pltpu.HBM)


def smem():
    return pl.BlockSpec(memory_space=pltpu.SMEM)


def queue_perm(move):
    def index(x, z, c):
        return (x * RING + z) * 2 + c

    return [
        (index(x, z, c), index(*move(x, z, c)))
        for x in range(2)
        for z in range(RING)
        for c in range(2)
    ]


UP = queue_perm(lambda x, z, c: (x, (z + 1) % RING, c))
DOWN = queue_perm(lambda x, z, c: (x, (z - 1) % RING, c))
CORE = queue_perm(lambda x, z, c: (x, z, 1 - c))


def start_all(pairs, sems):
    copies = [
        pltpu.make_async_copy(source, target, sems.at[i])
        for i, (source, target) in enumerate(pairs)
    ]
    for copy in copies:
        copy.start()
    return copies


def slot_spans(rows, z):
    return [
        pl.ds(pl.multiple_of(lax.rem(z + offset + RING, RING) * rows, rows), rows)
        for offset in GATHER
    ]


def unpack_ids(codes, wanted):
    values = codes[...].astype(F32)
    wanted[...] = jnp.broadcast_to(values[:, 0:1] * 128.0 + values[:, 1:2], wanted.shape)


def key_pairs(keys, held):
    pairs, start = [], 0
    for source in keys:
        pairs.append((source, held.at[pl.ds(start, source.shape[0]), :]))
        start += source.shape[0]
    return pairs


def picked_kernel(rows, first, place, *refs):
    slots, keys, out = refs[:RING], refs[RING:-6], refs[-6]
    held, codes, wanted, chosen, sems = refs[-5:]
    width, count = out.shape[1], held.shape[0] // 2
    spans = slot_spans(rows, place[0])
    pairs = [
        (slot.at[:, pl.ds(width, 128)], codes.at[span, :]) for slot, span in zip(slots, spans)
    ]
    copies = start_all(pairs + key_pairs(keys, held), sems)
    for copy in copies[:RING]:
        copy.wait()
    copies = copies[RING:]
    unpack_ids(codes, wanted)
    lane = lax.broadcasted_iota(jnp.int32, (BLOCK, 128), 1)
    for b in range(RING * rows // BLOCK):
        span = slice(b * BLOCK, (b + 1) * BLOCK)
        ids = wanted[span, 0:1].astype(jnp.int32)
        total = None
        for j in range(2):
            local = ids - place[3 + first + j]
            for g in range(count // 128):
                mine = lane == local - g * 128
                start = j * count + g * 128
                chosen[span, start : start + 128] = mine.astype(F32).astype(BF16)
            if b == 0:
                share = len(keys) // 2
                for copy in copies[j * share : (j + 1) * share]:
                    copy.wait()
            block = slice(j * count, (j + 1) * count)
            part = jnp.dot(chosen[span, block], held[block, :], preferred_element_type=F32)
            total = part if total is None else total + part
        out[span, :] = total.astype(BF16)


def attend(factor, first, place, queries, wanted, held, scores, probs, peaks, table, keep):
    count = held.shape[0] // 2

    def score(b):
        span = slice(b * BLOCK, (b + 1) * BLOCK)
        top = None
        for j in range(2):
            product = (
                lax.dot_general(
                    queries[span, :],
                    held[j * count : (j + 1) * count, :],
                    (((1,), (1,)), ((), ())),
                    preferred_element_type=F32,
                )
                * factor
            )
            scores[span, j * count : (j + 1) * count] = product
            for g in range(count // 128):
                part = product[:, g * 128 : (g + 1) * 128]
                top = part if top is None else jnp.maximum(top, part)
        peaks[span, :] = top

    def soften(b):
        size = 32
        lane = lax.broadcasted_iota(jnp.int32, (size, 128), 1)
        for q in range(BLOCK // size):
            span = slice(b * BLOCK + q * size, b * BLOCK + (q + 1) * size)
            peak = jnp.max(peaks[span, :], axis=1, keepdims=True)
            ids = wanted[span, 0:1].astype(jnp.int32)
            partial = jnp.zeros((size, 128), F32)
            found = jnp.zeros((size, 128), F32)
            for j in range(2):
                local = ids - place[3 + first + j]
                for g in range(count // 128):
                    columns = slice(j * count + g * 128, j * count + (g + 1) * 128)
                    values = scores[span, columns]
                    powers = jnp.exp(values - peak)
                    probs[span, columns] = powers.astype(BF16)
                    partial += powers
                    found += jnp.where(lane == local - g * 128, values, 0.0)
            total = jnp.sum(partial, axis=1, keepdims=True)
            score_here = jnp.sum(found, axis=1, keepdims=True)
            table[span, :] = jnp.where(
                lane == 0, peak, jnp.where(lane == 1, total, score_here)
            )

    def gather(b):
        span = slice(b * BLOCK, (b + 1) * BLOCK)
        total = None
        for j in range(2):
            block = slice(j * count, (j + 1) * count)
            part = jnp.dot(probs[span, block], held[block, :], preferred_element_type=F32)
            total = part if total is None else total + part
        keep(span, total)

    blocks = queries.shape[0] // BLOCK
    score(0)
    for b in range(blocks):
        if b + 1 < blocks:
            score(b + 1)
        soften(b)
        gather(b)


def near_kernel(factor, rows, place, *refs):
    slots = refs[:RING]
    own_weight, near_weight = refs[RING], refs[RING + 1 : RING + 6]
    keys, gain = refs[RING + 6 : RING + 8], refs[RING + 8]
    sums, table, queries, wanted, own_hidden, full_weight = refs[RING + 9 : RING + 15]
    speech, hidden, scores, probs, codes, peaks, held, sems = refs[RING + 15 :]
    z, mp, core = place[0], place[1], place[2]
    width = hidden.shape[1]
    piece = own_weight.shape[1]
    spans = slot_spans(rows, z)

    def column(step):
        start = pl.multiple_of(jnp.bitwise_xor(mp, step) * piece, piece)
        return full_weight.at[:, pl.ds(start, piece)]

    pairs = []
    for slot, span in zip(slots, spans):
        pairs.append((slot.at[:, pl.ds(0, width)], speech.at[span, :]))
        pairs.append((slot.at[:, pl.ds(width, 128)], codes.at[span, :]))
    pairs += [(own_weight, column(0)), (near_weight[3], column(4))]
    for i in range(3):
        pairs.append((near_weight[i], column(i + 1 + 4 * core)))
        pairs.append((near_weight[4].at[pl.ds(i * width, width), :], column(i + 5 - 4 * core)))
    first = len(pairs)
    copies = start_all(pairs + key_pairs(keys, held), sems)
    for copy in copies[:first]:
        copy.wait()
    unpack_ids(codes, wanted)

    hidden[...] = jnp.dot(speech[...], full_weight[...], preferred_element_type=F32)

    @pl.loop(0, RING)
    def _(b):
        span = pl.ds(pl.multiple_of(b * rows, rows), rows)
        block = hidden[span, :]
        inverse = lax.rsqrt(jnp.mean(block * block, axis=1, keepdims=True) + 1e-06)
        queries[span, :] = (block * inverse * gain[...]).astype(BF16)

    own_hidden[...] = hidden[pl.ds(pl.multiple_of(z * rows, rows), rows), :]
    for copy in copies[first:]:
        copy.wait()

    def keep(span, total):
        sums[span, :] = total

    attend(factor, 0, place, queries, wanted, held, scores, probs, peaks, table, keep)


def far_kernel(factor, place, *refs):
    keys, inputs = refs[:4], refs[4:8]
    sums, stats = refs[8], refs[9]
    scores, probs, peaks, table, held, queries, wanted, before, near_sums, sems = refs[10:]
    holders = (queries, wanted, before, near_sums)
    pairs = list(zip(inputs, holders)) + key_pairs(keys, held)
    for copy in start_all(pairs, sems):
        copy.wait()

    def keep(span, total):
        near, far = before[span, :], table[span, :]
        peak = jnp.maximum(near[:, 0:1], far[:, 0:1])
        left, right = jnp.exp(near[:, 0:1] - peak), jnp.exp(far[:, 0:1] - peak)
        sums[span, :] = near_sums[span, :] * left + total * right
        lane = lax.broadcasted_iota(jnp.int32, near.shape, 1)
        table[span, :] = jnp.where(
            lane == 0, peak, jnp.where(lane == 1, near * left + far * right, near + far)
        )

    attend(factor, 2, place, queries, wanted, held, scores, probs, peaks, table, keep)
    stats[...] = table[...].T[:8, :]


def join_kernel(count, *refs):
    parts, out = refs[:count], refs[count]
    peak = parts[0][0:1, :]
    for part in parts[1:]:
        peak = jnp.maximum(peak, part[0:1, :])
    total = found = 0.0
    for part in parts:
        total += part[1:2, :] * jnp.exp(part[0:1, :] - peak)
        found += part[2:3, :]
    row = lax.broadcasted_iota(jnp.int32, out.shape, 0)
    out[...] = jnp.where(row == 0, peak, jnp.where(row == 1, total, found))


def scale_kernel(rows, place, sums, near_picked, far_picked, local, merged, *refs):
    outs, loss, table = refs[:RING], refs[RING], refs[RING + 1]
    log_total = merged[0:1, :] + jnp.log(merged[1:2, :])
    scale = jnp.exp(local[0:1, :] - log_total)
    losses = log_total - merged[2:3, :]
    row = lax.broadcasted_iota(jnp.int32, (128, scale.shape[1]), 0)
    table[...] = jnp.where(row == 0, scale, losses).T

    def span_of(offset):
        start = lax.rem(place[0] + offset + RING, RING) * rows
        return pl.ds(pl.multiple_of(start, rows), rows)

    for slot, offset in enumerate(REDUCE):
        span = span_of(offset)
        picked = near_picked[span, :].astype(F32) + far_picked[span, :].astype(F32)
        outs[slot][...] = (table[span, 0:1] * sums[span, :] - picked).astype(BF16)
    own = jnp.broadcast_to(table[span_of(0), 1:2], (rows, 128))
    loss[...] = own.T[:1, :]


def add_kernel(first, second, out):
    out[...] = (first[...].astype(F32) + second[...].astype(F32)).astype(BF16)


def final_kernel(factor, first, second, own, hidden, gain, weight, out):
    width = hidden.shape[1]
    grad = (first[...].astype(F32) + second[...].astype(F32) + own[...].astype(F32)) * factor
    scaled = gain[...] * grad
    values = hidden[...]
    inverse = lax.rsqrt(jnp.mean(values * values, axis=1, keepdims=True) + 1e-06)
    inner = jnp.sum(scaled * values, axis=1, keepdims=True)
    hidden_grad = (
        inverse * scaled - values * (inverse * inverse * inverse) * inner / width
    ).astype(BF16)
    out[...] = lax.dot_general(
        hidden_grad, weight[...], (((1,), (1,)), ((), ())), preferred_element_type=F32
    ).astype(BF16)


def queue_kernel(shift, keys, fresh, out):
    count = keys.shape[0]
    wanted = lax.broadcasted_iota(jnp.int32, (count, 1), 0) + shift[0]
    pick = lax.broadcasted_iota(jnp.int32, (count, fresh.shape[0]), 1) == wanted
    moved = jnp.dot(pick.astype(F32).astype(BF16), fresh[...], preferred_element_type=F32)
    replaced = (wanted >= 0) & (wanted < fresh.shape[0])
    out[...] = jnp.where(replaced, moved, keys[...].astype(F32)).astype(BF16)


def shards(speech, weight, norm_gain, queue_keys, new_keys, pointer, positives):
    rows, width = speech.shape
    count = queue_keys.shape[0]
    total_rows = RING * rows
    queue_length = count * lax.axis_size("queue")
    queue_index = lax.axis_index("queue")
    mp = lax.axis_index("mp")
    z = (queue_index // 2) % RING
    factor = 2.0 / math.sqrt(width)

    core = queue_index % 2
    half = RING * 2
    across = [
        (q * 8 + m, (q ^ half) * 8 + (m ^ 4)) for q in range(4 * RING) for m in range(8)
    ]
    part = count // 2
    far_first = lax.ppermute(queue_keys[:part], ("queue", "mp"), across)
    far_last = lax.ppermute(queue_keys[part:], ("queue", "mp"), across)
    near = lax.ppermute(queue_keys, "queue", CORE)
    flipped = queue_index ^ (2 * RING)
    bases = [index * count for index in (queue_index, queue_index ^ 1, flipped, flipped ^ 1)]
    place = jnp.stack([z, mp, core] + bases).astype(jnp.int32)

    codes = jnp.stack([positives // 128, positives % 128], axis=1).astype(BF16)
    packed = jnp.concatenate([speech, jnp.pad(codes, ((0, 0), (0, 126)))], axis=1)
    slots = {0: packed}
    up = down = packed
    pieces, shard = [], weight
    for step in range(1, 5):
        shares = [(m ^ step, m ^ (step + 4) if step < 4 else m ^ step) for m in range(8)]
        moves = [
            (shares[m][q % 2] + q * 8, m + q * 8) for q in range(4 * RING) for m in range(8)
        ]
        piece = lax.ppermute(shard, ("queue", "mp"), moves)
        up = lax.ppermute(up, "queue", UP)
        if step < 4:
            down = lax.ppermute(down, "queue", DOWN)
            if step == 2:
                near, up = lax.optimization_barrier((near, up))
            piece, up, down, shard = lax.optimization_barrier((piece, up, down, weight))
            if step == 2:
                far_first, up, shard = lax.optimization_barrier((far_first, up, shard))
            slots[step] = down
        slots[-step] = up
        pieces.append(piece)
        if step == 3:
            other_pieces = lax.ppermute(jnp.concatenate(pieces, axis=0), "queue", CORE)
    gathered = [slots[offset] for offset in GATHER]
    far_first, *_ = lax.optimization_barrier((far_first, slots[-4], pieces[3], other_pieces))
    far_near_first = lax.ppermute(far_first, "queue", CORE)

    def pick(pair, first, place):
        return pl.pallas_call(
            functools.partial(picked_kernel, rows, first),
            out_shape=jax.ShapeDtypeStruct((total_rows, width), BF16),
            in_specs=[smem()] + [hbm()] * (RING + len(pair)),
            out_specs=vmem(),
            scratch_shapes=[
                pltpu.VMEM((2 * count, width), BF16),
                pltpu.VMEM((total_rows, 128), BF16),
                pltpu.VMEM((total_rows, 128), F32),
                pltpu.VMEM((total_rows, 2 * count), BF16),
                pltpu.SemaphoreType.DMA((RING + len(pair),)),
            ],
            compiler_params=limit(50),
            cost_estimate=pl.CostEstimate(
                flops=first * total_rows * width * count, bytes_accessed=1000, transcendentals=0
            ),
            name="picked",
        )(place, *gathered, *pair)

    gain = norm_gain.reshape(1, width)
    full = jax.ShapeDtypeStruct((total_rows, width), F32)
    narrow = jax.ShapeDtypeStruct((total_rows, 128), F32)
    near_sums, near_table, queries, wanted, own_hidden, full_weight = pl.pallas_call(
        functools.partial(near_kernel, factor, rows),
        out_shape=(
            full,
            narrow,
            jax.ShapeDtypeStruct((total_rows, width), BF16),
            narrow,
            jax.ShapeDtypeStruct((rows, width), F32),
            jax.ShapeDtypeStruct((width, width), BF16),
        ),
        in_specs=[smem()] + [hbm()] * (RING + 8) + [vmem()],
        out_specs=(vmem(),) * 6,
        scratch_shapes=[
            pltpu.VMEM((total_rows, width), BF16),
            pltpu.VMEM((total_rows, width), F32),
            pltpu.VMEM((total_rows, 2 * count), F32),
            pltpu.VMEM((total_rows, 2 * count), BF16),
            pltpu.VMEM((total_rows, 128), BF16),
            pltpu.VMEM((total_rows, 128), F32),
            pltpu.VMEM((2 * count, width), BF16),
            pltpu.SemaphoreType.DMA((2 * RING + 10,)),
        ],
        compiler_params=limit(50),
        cost_estimate=pl.CostEstimate(flops=1000, bytes_accessed=1000, transcendentals=0),
        name="near",
    )(place, *gathered, weight, *pieces, other_pieces, queue_keys, near, gain)

    far_last, near_table = lax.optimization_barrier((far_last, near_table))
    far_keys = (far_first, far_last, far_near_first, lax.ppermute(far_last, "queue", CORE))
    sums, stats = pl.pallas_call(
        functools.partial(far_kernel, factor),
        out_shape=(full, jax.ShapeDtypeStruct((8, total_rows), F32)),
        in_specs=[smem()] + [hbm()] * 8,
        out_specs=(vmem(),) * 2,
        scratch_shapes=[
            pltpu.VMEM((total_rows, 2 * count), F32),
            pltpu.VMEM((total_rows, 2 * count), BF16),
            pltpu.VMEM((total_rows, 128), F32),
            pltpu.VMEM((total_rows, 128), F32),
            pltpu.VMEM((2 * count, width), BF16),
            pltpu.VMEM((total_rows, width), BF16),
            pltpu.VMEM((total_rows, 128), F32),
            pltpu.VMEM((total_rows, 128), F32),
            pltpu.VMEM((total_rows, width), F32),
            pltpu.SemaphoreType.DMA((8,)),
        ],
        compiler_params=limit(50),
        cost_estimate=pl.CostEstimate(
            flops=8 * total_rows * width * count,
            bytes_accessed=12_000_000,
            transcendentals=total_rows * 2 * count,
        ),
        name="far",
    )(place, *far_keys, queries, wanted, near_table, near_sums)

    def join(*parts):
        return pl.pallas_call(
            functools.partial(join_kernel, len(parts)),
            out_shape=jax.ShapeDtypeStruct(stats.shape, F32),
            in_specs=[vmem()] * len(parts),
            out_specs=vmem(),
            compiler_params=limit(2),
            name="join",
        )(*parts)

    def swap(values, step):
        return lax.ppermute(values, "queue", queue_perm(lambda x, z, c: (x, z ^ step, c)))

    later, stats = lax.optimization_barrier((place, stats))
    other = swap(stats, 1)
    far_picked = pick(far_keys, 2, later)
    other, far_picked = lax.optimization_barrier((other, far_picked))
    pair = join(stats, other)
    later, pair = lax.optimization_barrier((later, pair))
    others = [swap(pair, step) for step in (2, 4, 6)]
    near_picked = pick((queue_keys, near), 0, later)
    near_picked, *others = lax.optimization_barrier((near_picked, *others))
    merged = join(pair, *others)

    *grads, losses = pl.pallas_call(
        functools.partial(scale_kernel, rows),
        out_shape=[jax.ShapeDtypeStruct((rows, width), BF16)] * RING
        + [jax.ShapeDtypeStruct((1, rows), F32)],
        in_specs=[smem()] + [vmem()] * 5,
        out_specs=[vmem()] * (RING + 1),
        scratch_shapes=[pltpu.VMEM((total_rows, 128), F32)],
        compiler_params=limit(16),
        cost_estimate=pl.CostEstimate(
            flops=3 * total_rows * width, bytes_accessed=6_000_000, transcendentals=2000
        ),
        name="scaled",
    )(place, sums, near_picked, far_picked, stats, merged)
    grads = dict(zip(REDUCE, grads))

    def add(first, second):
        return pl.pallas_call(
            add_kernel,
            out_shape=jax.ShapeDtypeStruct((rows, width), BF16),
            in_specs=[vmem()] * 2,
            out_specs=vmem(),
            compiler_params=limit(4),
            cost_estimate=pl.CostEstimate(
                flops=rows * width, bytes_accessed=600_000, transcendentals=0
            ),
            name="add",
        )(first, second)

    shift = (queue_index * count - pointer) % queue_length
    shift = jnp.where(shift >= queue_length - count, shift - queue_length, shift)
    fresh, grads[0] = lax.optimization_barrier((new_keys, grads[0]))
    queue_next = pl.pallas_call(
        queue_kernel,
        out_shape=jax.ShapeDtypeStruct(queue_keys.shape, BF16),
        in_specs=[smem(), vmem(), vmem()],
        out_specs=vmem(),
        compiler_params=limit(12),
        cost_estimate=pl.CostEstimate(
            flops=2 * count * count * width, bytes_accessed=5_000_000, transcendentals=0
        ),
        name="queue",
    )(shift, queue_keys, fresh)

    first, second = grads[4], grads[-3]
    for step in range(4):
        first = lax.ppermute(first, "queue", UP)
        if step == 0:
            first, queue_next = lax.optimization_barrier((first, queue_next))
        if step < 3:
            first = add(first, grads[3 - step])
            second = lax.ppermute(second, "queue", DOWN)
            if step < 2:
                second = add(second, grads[step - 2])

    grad_speech = pl.pallas_call(
        functools.partial(final_kernel, 16.0 * factor),
        out_shape=jax.ShapeDtypeStruct((rows, width), BF16),
        in_specs=[vmem()] * 6,
        out_specs=vmem(),
        compiler_params=limit(8),
        cost_estimate=pl.CostEstimate(
            flops=2 * rows * width * width, bytes_accessed=3_500_000, transcendentals=rows
        ),
        name="final",
    )(first, second, grads[0], own_hidden, gain, full_weight)
    return (losses.reshape(rows), grad_speech, queue_next)


def solution(mesh):
    return jax.shard_map(
        shards,
        mesh=mesh,
        in_specs=(
            P(("queue", "mp"), None),
            P(None, "mp"),
            P(),
            P("queue", None),
            P(),
            P(),
            P(("queue", "mp")),
        ),
        out_specs=(P(("queue", "mp")), P(("queue", "mp"), None), P("queue", None)),
        check_vma=False,
    )
```
